32 devices in a mesh: dp: 2 (over y), expert: 16 (over z, x, core).
Axes of the slice: x: 2, y: 2, z: 4, core: 2. Of those that a mesh axis runs over, the one named last changes fastest.
Arguments:
- tokens: bfloat16 [2048, 3584], P('expert', 'dp'), may hold values from -6 to 6
- cotangent: bfloat16 [2048, 3584], P('expert', 'dp'), may hold values from -12 to 12
- expert_ids: int32 [2048, 8], P('expert'), may hold values from 0 to 15, all different within a row; in each aligned block of 128 rows (0 to 127, 128 to 255, ...) at most 64 rows name the same one
- gate_levels: int32 [2048, 8], P('expert'), may hold values from 1 to 15
- capacity: int32 [16], replicated, may hold values from 16 to 64, as said below
- up_weight: bfloat16 [16, 3584, 1024], P('expert', 'dp'), may hold values from -0.09375 to 0.09375
- down_weight: bfloat16 [16, 3584, 1024], P('expert', 'dp'), may hold values from -0.1875 to 0.1875
Outputs:
- token_grad: bfloat16 [2048, 3584], P('expert', 'dp')
- up_grad: bfloat16 [16, 3584, 1024], P('expert', 'dp')
- down_grad: bfloat16 [16, 3584, 1024], P('expert', 'dp')
The draws below stay inside these ranges and needn't reach their ends.
Inputs may be any that keep to these rules, and one draw needn't show every extreme that they name: `expert_ids`: in each aligned block of 128 tokens every expert is named by exactly 64 choices. `capacity`: some expert accepts 64 rows and some only 4.
All inputs are finite; a program needn't handle non-finite values.
Results may differ from the reference program's by a relative error of at most 0.023.
Values may be sent and summed in bfloat16 or wider, within the bound.
No kernel may reach another device: no remote copies, remote signals or barrier semaphores. Data moves between devices by JAX's collectives and lax.ppermute only.
A program may use at most 64 MiB of HBM per device.

```python
import math
import jax
import jax.numpy as jnp
import numpy as np
from jax import lax

D = 3584
HW = 1024
TOP = 8
TOK_DEV = 128
EXPERTS = 16
TOKENS = 2048
CAP = 64
N_DP = 2
N_EXPERT = 16


def draw_capacity(key, part):
    least = (CAP + 3) // 4
    values = jax.random.randint(key, (EXPERTS,), least, CAP + 1)
    order = jax.random.permutation(jax.random.fold_in(key, 7), EXPERTS)
    values = values.at[order[0]].set(CAP)
    values = values.at[order[1]].set(least)
    return values.astype(jnp.int32)


def with_ends(array, rng, low, top_value):
    index_at = [jax.random.randint(jax.random.fold_in(rng, axis), (), 0, length) for axis, length in enumerate(array.shape)]
    longest = array.shape.index(max(array.shape))
    next_to = index_at[:longest] + [(index_at[longest] + 1) % array.shape[longest]] + index_at[longest + 1:]
    return array.at[tuple(index_at)].set(low).at[tuple(next_to)].set(top_value)


def level_of(key, extent, shards, smallest, high):
    factor_of, own = 1.0, jax.random.fold_in(key, 6)
    for dim, parts in shards:
        heights = jnp.exp(jax.random.uniform(jax.random.fold_in(own, dim), (parts,), jnp.float32, smallest / len(shards), high / len(shards)))
        factor_of = factor_of * jnp.repeat(heights, extent[dim] // parts).reshape([-1 if axis == dim else 1 for axis in range(len(extent))])
    return factor_of


def assign_block(stream_key, own, number, rows, count, top, most, skew):
    sequence = jax.random.permutation(stream_key, count)
    packed, common = shares(count, rows * top, most, skew, True), shares(count, rows * top, most, skew, False)
    places = jnp.arange(count)

    def named(sizes, offset_by):
        used = int((sizes > 0).sum())
        fixed = max(1, used // 4)
        moved = fixed + (places - fixed + offset_by * (used - fixed)) % max(1, count - fixed)
        return jnp.zeros((count,), jnp.int32).at[sequence[jnp.where(places < fixed, places, moved)]].set(jnp.asarray(sizes, jnp.int32))

    sizes = jnp.where(number % 4 == 0, named(packed, number // 4), named(common, number - number // 4 - 1))
    mixed = jax.random.permutation(jax.random.fold_in(own, 3), count)
    source_of, receiver = mixed[0:count // 2 * 2:2], mixed[1:count // 2 * 2:2]
    margin = jnp.minimum(sizes[source_of] - 1, most - sizes[receiver]) // 2
    margin = jnp.where((source_of == sequence[0]) | (receiver == sequence[0]) | (sizes[receiver] == 0), 0, jnp.maximum(margin, 0))
    moved = jax.random.randint(jax.random.fold_in(own, 4), (count // 2,), 0, 1 << 20) % (margin + 1)
    sizes = sizes.at[source_of].add(-moved).at[receiver].add(moved)
    items = jnp.searchsorted(jnp.cumsum(sizes), jnp.arange(rows * top), side="right").astype(jnp.int32)
    grid = items.reshape(top, rows).T
    grid = grid[jax.random.permutation(jax.random.fold_in(own, 1), rows)]
    offset_by = jax.random.randint(jax.random.fold_in(own, 2), (rows, 1), 0, top)
    return jnp.take_along_axis(grid, (jnp.arange(top)[None, :] + offset_by) % top, axis=1)


def shares(count, total, bound, skew, full):
    weights = [(1 << 20) // math.isqrt(grade ** skew) + 1 for grade in range(1, count + 1)]
    largest = bound if full else min(bound, max(-(-total // count), total * weights[0] // sum(weights)))
    least = 1 if total - largest >= count - 1 else 0
    counts, surplus = [largest] + [least] * (count - 1), total - largest - least * (count - 1)
    while surplus > 0:
        movable = [i for i in range(1, count) if counts[i] < largest] or [i for i in range(1, count) if counts[i] < bound]
        whole, remaining = sum([weights[i] for i in movable]), surplus
        for i in movable:
            addition = min(bound - counts[i], max(1, remaining * weights[i] // whole), surplus)
            counts[i] = counts[i] + addition
            surplus = surplus - addition
    return np.array(counts)


def bell_draw(stream_key, extent, scale, most, cuts=(), kind=jnp.bfloat16):
    entries = jax.random.normal(stream_key, extent, jnp.float32) * scale
    if len(cuts) > 0:
        entries = level_of(stream_key, extent, cuts, -0.22, 0.18) * entries
    return jnp.clip(entries, min=-most, max=most).astype(kind)


def setup_inputs(seed: int = 0) -> dict:
    keys = jax.random.split(jax.random.key(seed), 8)
    tokens = bell_draw(keys[0], (TOKENS, D), 1.0, 6.0, ((0, 16), (1, 2)))
    cotangent = bell_draw(keys[1], (TOKENS, D), 2.0, 12.0, ((0, 16), (1, 2)))
    expert_ids_keys = jax.random.split(jax.random.fold_in(keys[2], 1), TOKENS // TOK_DEV)
    expert_ids_turns = jax.random.permutation(jax.random.fold_in(keys[2], 3), TOKENS // TOK_DEV)
    expert_ids = jax.vmap(lambda own, number: assign_block(jax.random.fold_in(keys[2], 2), own, number, TOK_DEV, EXPERTS, TOP, CAP, 0))(expert_ids_keys, expert_ids_turns).reshape((TOKENS, TOP))
    gate_levels = with_ends(jax.random.randint(keys[3], (TOKENS, TOP), 1, 16), jax.random.fold_in(keys[3], 1), 1, 15).astype(jnp.int32)
    capacity = draw_capacity(jax.random.fold_in(keys[7], 71), 0)
    up_weight = bell_draw(keys[5], (EXPERTS, D, HW), D ** -0.5, 0.09375, ((0, 16), (1, 2)))
    down_weight = bell_draw(keys[6], (EXPERTS, D, HW), HW ** -0.5, 0.1875, ((0, 16), (1, 2)))
    return dict(tokens=tokens, cotangent=cotangent, expert_ids=expert_ids, gate_levels=gate_levels, capacity=capacity, up_weight=up_weight, down_weight=down_weight)


def silu_slope(preact):
    sigmoid = jax.nn.sigmoid(preact)
    return sigmoid * (1.0 + preact * (1.0 - sigmoid))


def grouped_partials(rows, weight):
    row_count = rows.shape[0]
    group_width = weight.shape[0] // N_DP
    rows_split = rows.astype(jnp.float32).reshape(row_count, N_DP, group_width)
    weight_split = weight.astype(jnp.float32).reshape(N_DP, group_width, weight.shape[1])
    partials = jnp.einsum('rpd,pdh->prh', rows_split, weight_split)
    rounded = lax.optimization_barrier(partials.astype(jnp.bfloat16))
    return jnp.sum(rounded.astype(jnp.float32), axis=0)


def reference(tokens, cotangent, expert_ids, gate_levels, capacity, up_weight, down_weight):
    num_blocks = N_EXPERT
    block_routes = TOK_DEV * TOP
    ids_blocks = expert_ids.reshape(num_blocks, block_routes)
    experts_row = jnp.arange(EXPERTS, dtype=jnp.int32)
    onehot = (ids_blocks[:, :, None] == experts_row[None, None, :]).astype(jnp.int32)
    earlier = jnp.cumsum(onehot, axis=1) - onehot
    slot_rank = jnp.sum(earlier * onehot, axis=2).astype(jnp.int32)
    kept_mask = (slot_rank < capacity[ids_blocks]).astype(jnp.int32)
    block_index = jnp.broadcast_to(jnp.arange(num_blocks, dtype=jnp.int32)[:, None], (num_blocks, block_routes))
    route_index = jnp.arange(num_blocks * block_routes, dtype=jnp.int32).reshape(num_blocks, block_routes)
    route_table = jnp.zeros((EXPERTS, num_blocks, CAP), jnp.int32).at[ids_blocks, block_index, slot_rank].set(route_index)
    mask_table = jnp.zeros((EXPERTS, num_blocks, CAP), jnp.int32).at[ids_blocks, block_index, slot_rank].set(kept_mask)
    levels = gate_levels.astype(jnp.float32)
    gate_weights = (levels / jnp.sum(levels, axis=1, keepdims=True)).reshape(-1)

    def per_expert(running, expert):
        routes = route_table[expert].reshape(-1)
        keep_rows = mask_table[expert].reshape(-1).astype(jnp.float32)
        token_index = (routes // TOP).astype(jnp.int32)
        expert_in = (tokens[token_index].astype(jnp.float32) * keep_rows[:, None]).astype(jnp.bfloat16)
        scaled = (gate_weights[routes][:, None] * cotangent[token_index].astype(jnp.float32)).astype(jnp.bfloat16)
        expert_cot = (scaled.astype(jnp.float32) * keep_rows[:, None]).astype(jnp.bfloat16)
        weight_up = up_weight[expert]
        weight_down = down_weight[expert]
        preact = grouped_partials(expert_in, weight_up)
        hidden_cot = grouped_partials(expert_cot, weight_down)
        hidden = jax.nn.silu(preact).astype(jnp.bfloat16)
        act_cot = (hidden_cot * silu_slope(preact)).astype(jnp.bfloat16)
        in_f32 = expert_in.astype(jnp.float32)
        cot_f32 = expert_cot.astype(jnp.float32)
        act_f32 = act_cot.astype(jnp.float32)
        grad_up = jnp.dot(in_f32.T, act_f32).astype(jnp.bfloat16)
        grad_down = jnp.dot(cot_f32.T, hidden.astype(jnp.float32)).astype(jnp.bfloat16)
        row_grad = jnp.dot(act_f32, weight_up.astype(jnp.float32).T).astype(jnp.bfloat16)
        running = running.at[token_index].add(row_grad.astype(jnp.float32))
        return running, (grad_up, grad_down)

    start_grad = jnp.zeros((TOKENS, D), jnp.float32)
    summed, grads = lax.scan(per_expert, start_grad, jnp.arange(EXPERTS, dtype=jnp.int32))
    return summed.astype(jnp.bfloat16), grads[0], grads[1]
```

```python
import functools

import jax
import jax.numpy as jnp
from jax import lax
from jax.sharding import PartitionSpec as P


def dot_f32(left, right, dims):
    return lax.dot_general(left, right, dims, preferred_element_type=jnp.float32)


def dp_sum(part, n_dp):
    part = part.astype(jnp.bfloat16)
    if n_dp == 2:
        other = lax.ppermute(part, "dp", [(0, 1), (1, 0)])
        return part.astype(jnp.float32) + other.astype(jnp.float32)
    return lax.psum(part.astype(jnp.float32), "dp")


def per_device(
    n_dp, n_expert, tokens, cotangent, expert_ids, gate_levels, capacity, up_weight, down_weight
):
    tok_rows, width_dev = tokens.shape
    top_count = expert_ids.shape[1]
    expert_count = capacity.shape[0]
    slots = tok_rows * top_count // expert_count
    row_count = n_expert * slots
    own = lax.axis_index("expert")

    routing = lax.all_gather(
        jnp.concatenate([expert_ids, gate_levels], axis=1), "expert", axis=0, tiled=True
    )
    tok_all = lax.all_gather(tokens, "expert", axis=0, tiled=False)
    cot_all = lax.all_gather(cotangent, "expert", axis=0, tiled=False)

    ids = routing[:, :top_count].reshape(n_expert, tok_rows, top_count)
    levels = routing[:, top_count:].reshape(n_expert, tok_rows, top_count).astype(jnp.float32)
    named = ids == own
    match = jnp.any(named, axis=2)
    gates = jnp.sum(jnp.where(named, levels, 0.0), axis=2) / jnp.sum(levels, axis=2)
    before = jnp.arange(tok_rows)[:, None] < jnp.arange(tok_rows)[None, :]
    rank = jnp.dot(
        match.astype(jnp.bfloat16), before.astype(jnp.bfloat16), preferred_element_type=jnp.float32
    ).astype(jnp.int32)
    kept = match & (rank < capacity[own])
    slot_of = jnp.where(kept, rank, -1)
    placing = slot_of[:, None, :] == jnp.arange(slots, dtype=jnp.int32)[None, :, None]
    slot_gate = jnp.sum(jnp.where(placing, gates[:, None, :], 0.0), axis=2)
    placing = placing.astype(jnp.bfloat16)

    pick = (((2,), (1,)), ((0,), (0,)))
    weight_up = up_weight[0]
    weight_down = down_weight[0]
    expert_in = dot_f32(placing, tok_all, pick).astype(jnp.bfloat16).reshape(row_count, width_dev)
    preact = dp_sum(jnp.dot(expert_in, weight_up, preferred_element_type=jnp.float32), n_dp)
    placed_cot = dot_f32(placing, cot_all, pick)
    expert_cot = (slot_gate[:, :, None] * placed_cot).astype(jnp.bfloat16)
    expert_cot = expert_cot.reshape(row_count, width_dev)
    hidden_cot = dp_sum(jnp.dot(expert_cot, weight_down, preferred_element_type=jnp.float32), n_dp)
    sigmoid = jax.nn.sigmoid(preact)
    hidden = (preact * sigmoid).astype(jnp.bfloat16)
    act_cot = (hidden_cot * (sigmoid * (1.0 + preact * (1.0 - sigmoid)))).astype(jnp.bfloat16)

    contract_rows = (((0,), (0,)), ((), ()))
    contract_hidden = (((1,), (1,)), ((), ()))
    back = dot_f32(act_cot, weight_up, contract_hidden).astype(jnp.bfloat16)
    back = back.reshape(n_expert, slots, width_dev)
    spread = dot_f32(placing, back, (((1,), (1,)), ((0,), (0,)))).astype(jnp.bfloat16)
    token_grad = lax.psum_scatter(
        spread.reshape(n_expert * tok_rows, width_dev), "expert", scatter_dimension=0, tiled=True
    )
    up_grad = dot_f32(expert_in, act_cot, contract_rows).astype(jnp.bfloat16)[None]
    down_grad = dot_f32(expert_cot, hidden, contract_rows).astype(jnp.bfloat16)[None]
    return (token_grad, up_grad, down_grad)


def solution(mesh):
    return jax.shard_map(
        functools.partial(per_device, mesh.shape["dp"], mesh.shape["expert"]),
        mesh=mesh,
        in_specs=(
            P("expert", "dp"),
            P("expert", "dp"),
            P("expert", None),
            P("expert", None),
            P(),
            P("expert", "dp", None),
            P("expert", "dp", None),
        ),
        out_specs=(P("expert", "dp"), P("expert", "dp", None), P("expert", "dp", None)),
        check_vma=False,
    )
```

```python
import functools

import jax
import jax.numpy as jnp
from jax import lax
from jax.experimental import pallas as pl
from jax.experimental.pallas import tpu as pltpu
from jax.sharding import PartitionSpec as P

F32 = jnp.float32
BF16 = jnp.bfloat16
CONTRACT_ROWS = (((0,), (0,)), ((), ()))
CONTRACT_LAST = (((1,), (1,)), ((), ()))

NZ, NX, NC = 4, 2, 2
ORDER = ((0, 1, 2, 3), (1, 0, 2, 3), (2, 3, 1, 0), (3, 2, 1, 0))


def dot_f32(left, right, dims=(((1,), (0,)), ((), ()))):
    return lax.dot_general(left, right, dims, preferred_element_type=F32)


def along_z(value, pairs):
    perm = [
        ((a * NX + x) * NC + c, (b * NX + x) * NC + c)
        for a, b in pairs
        for x in range(NX)
        for c in range(NC)
    ]
    return lax.ppermute(value, "expert", perm)


def swap_x(value):
    return lax.ppermute(value, "expert", [(i, i ^ NC) for i in range(NZ * NX * NC)])


def swap_core(value):
    return lax.ppermute(value, "expert", [(i, i ^ 1) for i in range(NZ * NX * NC)])


def swap_dp(value):
    return lax.ppermute(value, "dp", [(0, 1), (1, 0)])


NEIGHBOUR = ((0, 1), (1, 0), (2, 3), (3, 2))
MIDDLE = ((1, 2), (2, 1))
OUTWARD = ((1, 0), (2, 3))
INWARD = ((0, 1), (3, 2))


def gather_groups(block, inner):
    near = along_z(block, NEIGHBOUR)
    across = along_z(block, MIDDLE)
    outer_two = along_z(across, OUTWARD)
    far = along_z(near, MIDDLE)
    outer_three = along_z(far, OUTWARD)
    columns = [
        block,
        near,
        jnp.where(inner, across, outer_two),
        jnp.where(inner, far, outer_three),
    ]
    groups = []
    for own in columns:
        other = swap_x(own)
        groups.append((own, swap_core(own), other, swap_core(other)))
    return groups


def add(left, right):
    return (left.astype(F32) + right.astype(F32)).astype(BF16)


def scatter_groups(keep, send):
    sums = [None] * NZ
    for s in reversed(range(NZ)):
        chip = add(keep[s], swap_core(send[s]))
        sums[s] = add(chip[0], swap_x(chip[1]))
    far = add(sums[3], along_z(sums[3], INWARD))
    near = add(sums[1], along_z(far, MIDDLE))
    across = add(sums[2], along_z(sums[2], INWARD))
    return (
        sums[0].astype(F32)
        + along_z(across, MIDDLE).astype(F32)
        + along_z(near, NEIGHBOUR).astype(F32)
    ).astype(BF16)


def placing_of(slot_row, slots):
    return slot_row == lax.broadcasted_iota(jnp.int32, (slots, slot_row.shape[1]), 0)


def front_kernel(scaled, slots, slot_ref, gate_ref, b0, b1, b2, b3, weight_ref, rows_ref, part_ref, total):
    step = pl.program_id(0)
    for index, block in enumerate((b0, b1, b2, b3)):
        hit = placing_of(slot_ref[index], slots)
        picked = dot_f32(jnp.where(hit, 1.0, 0.0).astype(BF16), block[...])
        if scaled:
            gate = jnp.sum(jnp.where(hit, gate_ref[index], 0.0), axis=1, keepdims=True)
            picked = picked * gate
        rows_ref[index * slots : (index + 1) * slots, :] = picked.astype(BF16)
    product = dot_f32(rows_ref[...], weight_ref[...])

    @pl.when(step == 0)
    def _():
        total[...] = product

    @pl.when(step > 0)
    def _():
        total[...] += product

    @pl.when(step == pl.num_programs(0) - 1)
    def _():
        part_ref[...] = total[...].astype(BF16)


def front(blocks, slot_of, gates, weight, slots, scaled):
    tok_rows, width = blocks[0].shape
    hidden = weight.shape[1]
    rows = 4 * slots
    tile = width // 2
    whole = pl.BlockSpec((4, 1, tok_rows), lambda k: (0, 0, 0))
    return pl.pallas_call(
        functools.partial(front_kernel, scaled, slots),
        grid=(width // tile,),
        in_specs=[whole, whole]
        + [pl.BlockSpec((tok_rows, tile), lambda k: (0, k))] * 4
        + [pl.BlockSpec((tile, hidden), lambda k: (k, 0))],
        out_specs=[
            pl.BlockSpec((rows, tile), lambda k: (0, k)),
            pl.BlockSpec((rows, hidden), lambda k: (0, 0)),
        ],
        out_shape=[
            jax.ShapeDtypeStruct((rows, width), BF16),
            jax.ShapeDtypeStruct((rows, hidden), BF16),
        ],
        scratch_shapes=[pltpu.VMEM((rows, hidden), F32)],
        compiler_params=pltpu.CompilerParams(vmem_limit_bytes=24 * 1024 * 1024),
        cost_estimate=pl.CostEstimate(
            flops=2 * rows * width * (hidden + tok_rows),
            bytes_accessed=2 * (width * hidden + 2 * rows * width + 4 * tok_rows * width),
            transcendentals=0,
        ),
    )(slot_of, gates, *blocks, weight)


def back_kernel(slots, slot_ref, pre_a, pre_b, cot_a, cot_b, weight_ref, hidden_ref, act_ref, keep_ref, send_ref):
    @pl.when(pl.program_id(0) == 0)
    def _():
        preact = pre_a[...].astype(F32) + pre_b[...].astype(F32)
        hidden_cot = cot_a[...].astype(F32) + cot_b[...].astype(F32)
        sigmoid = jax.nn.sigmoid(preact)
        hidden_ref[...] = (preact * sigmoid).astype(BF16)
        act_ref[...] = (hidden_cot * (sigmoid * (1.0 + preact * (1.0 - sigmoid)))).astype(BF16)

    back = dot_f32(act_ref[...], weight_ref[...], CONTRACT_LAST).astype(BF16)
    for index in range(4):
        hit = placing_of(slot_ref[index], slots)
        placing = jnp.where(hit, 1.0, 0.0).astype(BF16)
        spread = dot_f32(placing, back[index * slots : (index + 1) * slots], CONTRACT_ROWS)
        out_ref = send_ref if index % 2 else keep_ref
        out_ref[index // 2] = spread.astype(BF16)


def back(slot_of, parts, weight, slots):
    tok_rows = slot_of.shape[2]
    width, hidden = weight.shape
    rows = 4 * slots
    tile = width // 2
    full = pl.BlockSpec((rows, hidden), lambda n: (0, 0))
    spread = pl.BlockSpec((2, tok_rows, tile), lambda n: (0, 0, n))
    return pl.pallas_call(
        functools.partial(back_kernel, slots),
        grid=(width // tile,),
        in_specs=[pl.BlockSpec((4, 1, tok_rows), lambda n: (0, 0, 0))]
        + [full] * 4
        + [pl.BlockSpec((tile, hidden), lambda n: (n, 0))],
        out_specs=[full, full, spread, spread],
        out_shape=[
            jax.ShapeDtypeStruct((rows, hidden), BF16),
            jax.ShapeDtypeStruct((rows, hidden), BF16),
            jax.ShapeDtypeStruct((2, tok_rows, width), BF16),
            jax.ShapeDtypeStruct((2, tok_rows, width), BF16),
        ],
        compiler_params=pltpu.CompilerParams(vmem_limit_bytes=32 * 1024 * 1024),
        cost_estimate=pl.CostEstimate(
            flops=2 * rows * width * (hidden + tok_rows),
            bytes_accessed=2 * (width * hidden + 6 * rows * hidden + 4 * tok_rows * width),
            transcendentals=rows * hidden,
        ),
    )(slot_of, *parts, weight)


def grad_kernel(*refs):
    out_ref = refs[-1]
    half = (len(refs) - 1) // 2
    total = None
    for left, right in zip(refs[:half], refs[half:-1]):
        term = dot_f32(left[...], right[...], CONTRACT_ROWS)
        total = term if total is None else total + term
    out_ref[...] = total.astype(BF16)


def grad(lefts, rights):
    rows, width = lefts[0].shape
    hidden = rights[0].shape[1]
    count = len(lefts)
    tile = 256
    return pl.pallas_call(
        grad_kernel,
        grid=(width // tile,),
        in_specs=[pl.BlockSpec((rows, tile), lambda n: (0, n))] * count
        + [pl.BlockSpec((rows, hidden), lambda n: (0, 0))] * count,
        out_specs=pl.BlockSpec((tile, hidden), lambda n: (n, 0)),
        out_shape=jax.ShapeDtypeStruct((width, hidden), BF16),
        compiler_params=pltpu.CompilerParams(vmem_limit_bytes=24 * 1024 * 1024),
        cost_estimate=pl.CostEstimate(
            flops=2 * count * rows * width * hidden,
            bytes_accessed=2 * (width * hidden + count * rows * (width + hidden)),
            transcendentals=0,
        ),
    )(*lefts, *rights)


def slots_and_gates(routing, own, limit, top_count):
    ids = routing[:, :, :top_count]
    levels = routing[:, :, top_count:].astype(F32)
    tok_rows = ids.shape[1]
    named = ids == own
    match = jnp.any(named, axis=2)
    gates = jnp.sum(jnp.where(named, levels, 0.0), axis=2) / jnp.sum(levels, axis=2)
    before = jnp.arange(tok_rows)[:, None] < jnp.arange(tok_rows)[None, :]
    rank = dot_f32(match.astype(BF16), before.astype(BF16)).astype(jnp.int32)
    return jnp.where(match & (rank < limit), rank, -1), gates


def grouped(tokens, cotangent, expert_ids, gate_levels, capacity, up_weight, down_weight):
    tok_rows, width = tokens.shape
    top_count = expert_ids.shape[1]
    slots = tok_rows * top_count // capacity.shape[0]
    own = lax.axis_index("expert")
    z, x, c = own // (NX * NC), (own // NC) % NX, own % NC
    inner = (z > 0) & (z < NZ - 1)
    weight_up, weight_down = up_weight[0], down_weight[0]

    routing = lax.all_gather(
        jnp.concatenate([expert_ids, gate_levels], axis=1), "expert", axis=0, tiled=False
    )
    order = jnp.array(ORDER, jnp.int32)[z]
    flip = jnp.arange(2, dtype=jnp.int32)
    block_ids = (order[:, None, None] * NX + (x ^ flip)[None, :, None]) * NC + (c ^ flip)
    slot_of, gates = slots_and_gates(routing, own, capacity[own], top_count)
    slot_of = slot_of[block_ids.reshape(-1)].reshape(NZ, 4, 1, tok_rows)
    gates = gates[block_ids.reshape(-1)].reshape(NZ, 4, 1, tok_rows)

    tok_groups = gather_groups(tokens, inner)
    cot_groups = gather_groups(cotangent, inner)
    rows_in, pre = [], []
    for s in range(NZ):
        rows, part = front(tok_groups[s], slot_of[s], gates[s], weight_up, slots, False)
        rows_in.append(rows)
        pre.append((part, swap_dp(part)))
    rows_cot, cot = [], []
    for s in range(NZ):
        rows, part = front(cot_groups[s], slot_of[s], gates[s], weight_down, slots, True)
        rows_cot.append(rows)
        cot.append((part, swap_dp(part)))
    hidden, act, keep, send = [], [], [], []
    for s in range(NZ):
        h, a, k, d = back(slot_of[s], pre[s] + cot[s], weight_up, slots)
        hidden.append(h)
        act.append(a)
        keep.append(k)
        send.append(d)
    token_grad = scatter_groups(keep, send)
    up_grad = grad(rows_in, act)[None]
    down_grad = grad(rows_cot, hidden)[None]
    return token_grad, up_grad, down_grad


def general(n_expert, tokens, cotangent, expert_ids, gate_levels, capacity, up_weight, down_weight):
    tok_rows, width = tokens.shape
    top_count = expert_ids.shape[1]
    slots = tok_rows * top_count // capacity.shape[0]
    row_count = n_expert * slots
    own = lax.axis_index("expert")
    weight_up, weight_down = up_weight[0], down_weight[0]

    routing = lax.all_gather(
        jnp.concatenate([expert_ids, gate_levels], axis=1), "expert", axis=0, tiled=False
    )
    tok_all = lax.all_gather(tokens, "expert", axis=0, tiled=False)
    cot_all = lax.all_gather(cotangent, "expert", axis=0, tiled=False)
    slot_of, gates = slots_and_gates(routing, own, capacity[own], top_count)
    placing = slot_of[:, None, :] == jnp.arange(slots, dtype=jnp.int32)[None, :, None]
    slot_gate = jnp.sum(jnp.where(placing, gates[:, None, :], 0.0), axis=2)
    placing = placing.astype(BF16)
    pick = (((2,), (1,)), ((0,), (0,)))
    rows_in = dot_f32(placing, tok_all, pick).astype(BF16).reshape(row_count, width)
    rows_cot = (slot_gate[:, :, None] * dot_f32(placing, cot_all, pick)).astype(BF16)
    rows_cot = rows_cot.reshape(row_count, width)
    preact = lax.psum(dot_f32(rows_in, weight_up).astype(BF16).astype(F32), "dp")
    hidden_cot = lax.psum(dot_f32(rows_cot, weight_down).astype(BF16).astype(F32), "dp")
    sigmoid = jax.nn.sigmoid(preact)
    hidden = (preact * sigmoid).astype(BF16)
    act = (hidden_cot * (sigmoid * (1.0 + preact * (1.0 - sigmoid)))).astype(BF16)
    row_grad = dot_f32(act, weight_up, CONTRACT_LAST).astype(BF16)
    spread = dot_f32(
        placing, row_grad.reshape(n_expert, slots, width), (((1,), (1,)), ((0,), (0,)))
    ).astype(BF16)
    token_grad = lax.psum_scatter(
        spread.reshape(n_expert * tok_rows, width), "expert", scatter_dimension=0, tiled=True
    )
    up_grad = dot_f32(rows_in, act, CONTRACT_ROWS).astype(BF16)[None]
    down_grad = dot_f32(rows_cot, hidden, CONTRACT_ROWS).astype(BF16)[None]
    return token_grad, up_grad, down_grad


def solution(mesh):
    n_dp, n_expert = mesh.shape["dp"], mesh.shape["expert"]
    if n_dp == 2 and n_expert == NZ * NX * NC:
        body = grouped
    else:
        body = functools.partial(general, n_expert)
    return jax.shard_map(
        body,
        mesh=mesh,
        in_specs=(
            P("expert", "dp"),
            P("expert", "dp"),
            P("expert", None),
            P("expert", None),
            P(),
            P("expert", "dp", None),
            P("expert", "dp", None),
        ),
        out_specs=(P("expert", "dp"), P("expert", "dp", None), P("expert", "dp", None)),
        check_vma=False,
    )
```

```python
import functools

import jax
import jax.numpy as jnp
from jax import lax
from jax.experimental import pallas as pl
from jax.experimental.pallas import tpu as pltpu
from jax.sharding import PartitionSpec as P

F32 = jnp.float32
BF16 = jnp.bfloat16
CONTRACT_ROWS = (((0,), (0,)), ((), ()))
CONTRACT_LAST = (((1,), (1,)), ((), ()))

NO_COST = pl.CostEstimate(flops=0, bytes_accessed=0, transcendentals=0)

NZ, NX, NC = 4, 2, 2


def dot_f32(left, right, dims=(((1,), (0,)), ((), ()))):
    return lax.dot_general(left, right, dims, preferred_element_type=F32)


def along_z(value, pairs):
    perm = [
        ((a * NX + x) * NC + c, (b * NX + x) * NC + c)
        for a, b in pairs
        for x in range(NX)
        for c in range(NC)
    ]
    return lax.ppermute(value, "expert", perm)


def swap_x(value):
    return lax.ppermute(value, "expert", [(i, i ^ NC) for i in range(NZ * NX * NC)])


def swap_core(value):
    return lax.ppermute(value, "expert", [(i, i ^ 1) for i in range(NZ * NX * NC)])


def swap_dp(value):
    return lax.ppermute(value, "dp", [(0, 1), (1, 0)])


NEIGHBOUR = ((0, 1), (1, 0), (2, 3), (3, 2))
MIDDLE = ((1, 2), (2, 1))
OUTWARD = ((1, 0), (2, 3))
INWARD = ((0, 1), (3, 2))


def tie(value, *earlier):
    return lax.optimization_barrier((value, earlier))[0]


def add(left, right):
    return (left.astype(F32) + right.astype(F32)).astype(BF16)


def placing_of(slot_row, slots):
    return slot_row == lax.broadcasted_iota(jnp.int32, (slots, slot_row.shape[1]), 0)


LANES = 128


def with_routing(tokens, expert_ids, gate_levels):
    half = LANES // 2
    room = ((0, 0), (0, half - expert_ids.shape[1]))
    parts = [tokens, jnp.pad(expert_ids, room).astype(BF16), jnp.pad(gate_levels, room).astype(BF16)]
    return jnp.concatenate(parts, axis=1)


def read_routing(meta, own, limit, top_count):
    tok_rows = meta.shape[0]
    ids = meta.astype(F32)
    levels = pltpu.roll(ids, LANES // 2, 1)
    choice = lax.broadcasted_iota(jnp.int32, ids.shape, 1) < top_count
    named = choice & (ids == own)
    ones = jnp.ones((8, LANES), BF16)
    match = dot_f32(ones, jnp.where(named, 1.0, 0.0).astype(BF16), CONTRACT_LAST)
    level = dot_f32(ones, jnp.where(named, levels, 0.0).astype(BF16), CONTRACT_LAST)
    total = dot_f32(ones, jnp.where(choice, levels, 0.0).astype(BF16), CONTRACT_LAST)
    square = (tok_rows, tok_rows)
    before = lax.broadcasted_iota(jnp.int32, square, 0) < lax.broadcasted_iota(jnp.int32, square, 1)
    rank = dot_f32(match.astype(BF16), jnp.where(before, 1.0, 0.0).astype(BF16))
    kept = (match > 0.5) & (rank < limit)
    return jnp.where(kept, rank, -1.0).astype(jnp.int32), level / total


def add_up(total, part_ref, product):
    step = pl.program_id(0)

    @pl.when(step == 0)
    def _():
        total[...] = product

    @pl.when(step > 0)
    def _():
        total[...] += product

    @pl.when(step == pl.num_programs(0) - 1)
    def _():
        part_ref[...] = total[...].astype(BF16)


def tokens_kernel(top_count, slots, own_ref, m0, m1, m2, m3, b0, b1, b2, b3, weight_ref, rows_ref, part_ref, slot_ref, gate_ref, total):
    @pl.when(pl.program_id(0) == 0)
    def _():
        own = own_ref[0].astype(F32)
        limit = own_ref[1].astype(F32)
        for index, meta in enumerate((m0, m1, m2, m3)):
            slot, gate = read_routing(meta[...], own, limit, top_count)
            slot_ref[index] = slot
            gate_ref[index] = gate

    for index, block in enumerate((b0, b1, b2, b3)):
        hit = placing_of(slot_ref[index, 0:1, :], slots)
        picked = dot_f32(jnp.where(hit, 1.0, 0.0).astype(BF16), block[...])
        rows_ref[index * slots : (index + 1) * slots, :] = picked.astype(BF16)
    add_up(total, part_ref, dot_f32(rows_ref[...], weight_ref[...]))


def cotangent_kernel(slots, slot_ref, gate_ref, b0, b1, b2, b3, weight_ref, rows_ref, part_ref, total):
    for index, block in enumerate((b0, b1, b2, b3)):
        hit = placing_of(slot_ref[index, 0:1, :], slots)
        picked = dot_f32(jnp.where(hit, 1.0, 0.0).astype(BF16), block[...])
        gate = jnp.sum(jnp.where(hit, gate_ref[index, 0:1, :], 0.0), axis=1, keepdims=True)
        rows_ref[index * slots : (index + 1) * slots, :] = (picked * gate).astype(BF16)
    add_up(total, part_ref, dot_f32(rows_ref[...], weight_ref[...]))


def front_specs(tok_rows, width, hidden, rows):
    tile = width // 2
    table = pl.BlockSpec((4, 8, tok_rows), lambda k: (0, 0, 0))
    blocks = [pl.BlockSpec((tok_rows, tile), lambda k: (0, k))] * 4
    weight = pl.BlockSpec((tile, hidden), lambda k: (k, 0))
    outs = [
        pl.BlockSpec((rows, tile), lambda k: (0, k)),
        pl.BlockSpec((rows, hidden), lambda k: (0, 0)),
    ]
    shapes = [jax.ShapeDtypeStruct((rows, width), BF16), jax.ShapeDtypeStruct((rows, hidden), BF16)]
    rest = dict(
        grid=(width // tile,),
        scratch_shapes=[pltpu.VMEM((rows, hidden), F32)],
        compiler_params=pltpu.CompilerParams(vmem_limit_bytes=24 * 1024 * 1024),
        cost_estimate=NO_COST,
    )
    return table, blocks, weight, outs, shapes, rest


def front_tokens(blocks, own, weight, slots, top_count):
    tok_rows = blocks[0].shape[0]
    width, hidden = weight.shape
    table, block_specs, weight_spec, outs, shapes, rest = front_specs(tok_rows, width, hidden, 4 * slots)
    meta = pl.BlockSpec((tok_rows, LANES), lambda k: (0, width // LANES))
    return pl.pallas_call(
        functools.partial(tokens_kernel, top_count, slots),
        in_specs=[pl.BlockSpec(memory_space=pltpu.SMEM)] + [meta] * 4 + block_specs + [weight_spec],
        out_specs=outs + [table, table],
        out_shape=shapes
        + [
            jax.ShapeDtypeStruct((4, 8, tok_rows), jnp.int32),
            jax.ShapeDtypeStruct((4, 8, tok_rows), F32),
        ],
        **rest,
    )(own, *blocks, *blocks, weight)


def front_cotangent(blocks, tables, weight, slots):
    tok_rows = blocks[0].shape[0]
    width, hidden = weight.shape
    table, block_specs, weight_spec, outs, shapes, rest = front_specs(tok_rows, width, hidden, 4 * slots)
    return pl.pallas_call(
        functools.partial(cotangent_kernel, slots),
        in_specs=[table, table] + block_specs + [weight_spec],
        out_specs=outs,
        out_shape=shapes,
        **rest,
    )(*tables, *blocks, weight)


def back_kernel(slots, slot_ref, pre_a, pre_b, cot_a, cot_b, weight_ref, act_ref, keep_ref, send_ref):
    @pl.when(pl.program_id(0) == 0)
    def _():
        preact = pre_a[...].astype(F32) + pre_b[...].astype(F32)
        hidden_cot = cot_a[...].astype(F32) + cot_b[...].astype(F32)
        sigmoid = jax.nn.sigmoid(preact)
        act_ref[...] = (hidden_cot * (sigmoid * (1.0 + preact * (1.0 - sigmoid)))).astype(BF16)

    back = dot_f32(act_ref[...], weight_ref[...], CONTRACT_LAST).astype(BF16)
    for index in range(4):
        hit = placing_of(slot_ref[index, 0:1, :], slots)
        placing = jnp.where(hit, 1.0, 0.0).astype(BF16)
        spread = dot_f32(placing, back[index * slots : (index + 1) * slots], CONTRACT_ROWS)
        out_ref = send_ref if index % 2 else keep_ref
        out_ref[index // 2] = spread.astype(BF16)


def back(slot_of, parts, weight, slots):
    tok_rows = slot_of.shape[2]
    width, hidden = weight.shape
    rows = 4 * slots
    tile = width // 2
    full = pl.BlockSpec((rows, hidden), lambda n: (0, 0))
    spread = pl.BlockSpec((2, tok_rows, tile), lambda n: (0, 0, n))
    return pl.pallas_call(
        functools.partial(back_kernel, slots),
        grid=(width // tile,),
        in_specs=[pl.BlockSpec((4, 8, tok_rows), lambda n: (0, 0, 0))]
        + [full] * 4
        + [pl.BlockSpec((tile, hidden), lambda n: (n, 0))],
        out_specs=[full, spread, spread],
        out_shape=[
            jax.ShapeDtypeStruct((rows, hidden), BF16),
            jax.ShapeDtypeStruct((2, tok_rows, width), BF16),
            jax.ShapeDtypeStruct((2, tok_rows, width), BF16),
        ],
        compiler_params=pltpu.CompilerParams(vmem_limit_bytes=32 * 1024 * 1024),
        cost_estimate=NO_COST,
    )(slot_of, *parts, weight)


def up_grad_kernel(*refs):
    count = (len(refs) - 1) // 2
    total = None
    for left, right in zip(refs[:count], refs[count:-1]):
        term = dot_f32(left[...], right[...], CONTRACT_ROWS)
        total = term if total is None else total + term
    refs[-1][...] = total.astype(BF16)


def down_grad_kernel(*refs):
    count = (len(refs) - 2) // 3
    out_ref, hidden_ref = refs[-2:]

    @pl.when(pl.program_id(0) == 0)
    def _():
        for index, (first, second) in enumerate(zip(refs[count : 2 * count], refs[2 * count : -2])):
            preact = first[...].astype(F32) + second[...].astype(F32)
            hidden_ref[index] = (preact * jax.nn.sigmoid(preact)).astype(BF16)

    total = None
    for index, left in enumerate(refs[:count]):
        term = dot_f32(left[...], hidden_ref[index], CONTRACT_ROWS)
        total = term if total is None else total + term
    out_ref[...] = total.astype(BF16)


def weight_grad(kernel, lefts, rights, scratch_shapes):
    rows, width = lefts[0].shape
    hidden = rights[0].shape[1]
    count = len(lefts)
    tile = 256
    return pl.pallas_call(
        kernel,
        grid=(width // tile,),
        in_specs=[pl.BlockSpec((rows, tile), lambda n: (0, n))] * count
        + [pl.BlockSpec((rows, hidden), lambda n: (0, 0))] * len(rights),
        out_specs=pl.BlockSpec((tile, hidden), lambda n: (n, 0)),
        out_shape=jax.ShapeDtypeStruct((width, hidden), BF16),
        scratch_shapes=scratch_shapes,
        compiler_params=pltpu.CompilerParams(vmem_limit_bytes=32 * 1024 * 1024),
        cost_estimate=NO_COST,
    )(*lefts, *rights)


def slots_and_gates(routing, own, limit, top_count):
    ids = routing[:, :, :top_count]
    levels = routing[:, :, top_count:].astype(F32)
    tok_rows = ids.shape[1]
    named = ids == own
    match = jnp.any(named, axis=2)
    gates = jnp.sum(jnp.where(named, levels, 0.0), axis=2) / jnp.sum(levels, axis=2)
    before = jnp.arange(tok_rows)[:, None] < jnp.arange(tok_rows)[None, :]
    rank = dot_f32(match.astype(BF16), before.astype(BF16)).astype(jnp.int32)
    return jnp.where(match & (rank < limit), rank, -1), gates


def grouped(tokens, cotangent, expert_ids, gate_levels, capacity, up_weight, down_weight):
    top_count = expert_ids.shape[1]
    slots = tokens.shape[0] * top_count // capacity.shape[0]
    own = lax.axis_index("expert")
    z = own // (NX * NC)
    inner = (z > 0) & (z < NZ - 1)
    who = jnp.stack([own.astype(jnp.int32), capacity[own]])
    weight_up, weight_down = up_weight[0], down_weight[0]

    rows_in, rows_cot, tables, pre, cot = ([None] * NZ for _ in range(5))

    def first(s, mine, mine_core, other):
        blocks = (mine, mine_core, other, swap_core(other))
        rows_in[s], part, slot, gate = front_tokens(blocks, who, weight_up, slots, top_count)
        tables[s] = (slot, gate)
        pre[s] = (part, swap_dp(part))

    def second(s, mine, mine_core, other):
        blocks = (mine, mine_core, other, swap_core(other))
        rows_cot[s], part = front_cotangent(blocks, tables[s], weight_down, slots)
        cot[s] = (part, swap_dp(part))

    tok = with_routing(tokens, expert_ids, gate_levels)
    x0 = swap_x(tok)
    near = along_z(tok, NEIGHBOUR)
    two_in = along_z(tok, MIDDLE)
    tok_core = swap_core(tok)

    near, two_in = tie((near, two_in), x0)
    x1 = swap_x(near)
    far_in = along_z(near, MIDDLE)
    two_out = along_z(two_in, OUTWARD)
    first(0, tok, tok_core, x0)

    two, far_in, cot_own = tie((jnp.where(inner, two_in, two_out), far_in, cotangent), x1, pre[0][0])
    x2 = swap_x(two)
    far_out = along_z(far_in, OUTWARD)
    cot_near_in = along_z(cot_own, INWARD)
    cot_two_in = along_z(cot_own, MIDDLE)
    first(1, near, swap_core(near), x1)

    far, cot_own, cot_near_in = tie(
        (jnp.where(inner, far_in, far_out), cot_own, cot_near_in), x2, pre[1][0], pre[0][1]
    )
    x3 = swap_x(far)
    cot_near_out = along_z(cot_own, OUTWARD)
    cot_far_in = along_z(cot_near_in, MIDDLE)
    first(2, two, swap_core(two), x2)

    cot_near, cot_far_in = tie(
        (jnp.where(inner, cot_near_in, cot_near_out), cot_far_in), x3, pre[2][0], pre[1][1]
    )
    x4 = swap_x(cot_near)
    cot_far_out = along_z(cot_far_in, OUTWARD)
    first(3, far, swap_core(far), x3)

    cot_far, cot_two_in = tie(
        (jnp.where(inner, cot_far_in, cot_far_out), cot_two_in), x4, pre[3][0], pre[2][1]
    )
    x5 = swap_x(cot_far)
    cot_two_out = along_z(cot_two_in, OUTWARD)
    second(1, cot_near, swap_core(cot_near), x4)

    cot_two = tie(jnp.where(inner, cot_two_in, cot_two_out), x5, cot[1][0], pre[3][1])
    x6 = swap_x(cot_two)
    second(3, cot_far, swap_core(cot_far), x5)

    cot_own = tie(cot_own, x6, cot[3][0], cot[1][1])
    x7 = swap_x(cot_own)
    second(2, cot_two, swap_core(cot_two), x6)

    act, chip = [None] * NZ, [None] * NZ

    def last(s):
        act[s], keep, send = back(tables[s][0], pre[s] + cot[s], weight_up, slots)
        chip[s] = add(keep, swap_core(send))

    last(1)
    near_send, cot_own = tie((chip[1][1], cot_own), x7, cot[2][0], cot[3][1])
    x8 = swap_x(near_send)
    second(0, cot_own, swap_core(cot_own), x7)
    last(3)

    far_send = tie(chip[3][1], x8, cot[0][0], cot[2][1])
    x9 = swap_x(far_send)
    last(2)

    two_send, far_sum = tie((chip[2][1], add(chip[3][0], x9)), cot[0][1])
    x10 = swap_x(two_send)
    hop_far = along_z(far_sum, INWARD)
    last(0)

    own_send, far_sum, two_sum = tie((chip[0][1], add(far_sum, hop_far), add(chip[2][0], x10)))
    x11 = swap_x(own_send)
    hop_far = along_z(far_sum, MIDDLE)
    hop_two = along_z(two_sum, INWARD)
    down_grad = weight_grad(
        down_grad_kernel,
        rows_cot,
        [p[0] for p in pre] + [p[1] for p in pre],
        [pltpu.VMEM((NZ,) + pre[0][0].shape, BF16)],
    )

    near_sum, two_sum = tie(
        (add(add(chip[1][0], x8), hop_far), add(two_sum, hop_two)), x11, down_grad
    )
    hop_near = along_z(near_sum, NEIGHBOUR)
    hop_two = along_z(two_sum, MIDDLE)
    up_grad = weight_grad(up_grad_kernel, rows_in, act, [])
    token_grad = (
        add(chip[0][0], x11).astype(F32) + hop_near.astype(F32) + hop_two.astype(F32)
    ).astype(BF16)
    return token_grad, up_grad[None], down_grad[None]


def general(n_expert, tokens, cotangent, expert_ids, gate_levels, capacity, up_weight, down_weight):
    tok_rows, width = tokens.shape
    top_count = expert_ids.shape[1]
    slots = tok_rows * top_count // capacity.shape[0]
    row_count = n_expert * slots
    own = lax.axis_index("expert")
    weight_up, weight_down = up_weight[0], down_weight[0]

    routing = lax.all_gather(
        jnp.concatenate([expert_ids, gate_levels], axis=1), "expert", axis=0, tiled=False
    )
    tok_all = lax.all_gather(tokens, "expert", axis=0, tiled=False)
    cot_all = lax.all_gather(cotangent, "expert", axis=0, tiled=False)
    slot_of, gates = slots_and_gates(routing, own, capacity[own], top_count)
    placing = slot_of[:, None, :] == jnp.arange(slots, dtype=jnp.int32)[None, :, None]
    slot_gate = jnp.sum(jnp.where(placing, gates[:, None, :], 0.0), axis=2)
    placing = placing.astype(BF16)
    pick = (((2,), (1,)), ((0,), (0,)))
    rows_in = dot_f32(placing, tok_all, pick).astype(BF16).reshape(row_count, width)
    rows_cot = (slot_gate[:, :, None] * dot_f32(placing, cot_all, pick)).astype(BF16)
    rows_cot = rows_cot.reshape(row_count, width)
    preact = lax.psum(dot_f32(rows_in, weight_up).astype(BF16).astype(F32), "dp")
    hidden_cot = lax.psum(dot_f32(rows_cot, weight_down).astype(BF16).astype(F32), "dp")
    sigmoid = jax.nn.sigmoid(preact)
    hidden = (preact * sigmoid).astype(BF16)
    act = (hidden_cot * (sigmoid * (1.0 + preact * (1.0 - sigmoid)))).astype(BF16)
    row_grad = dot_f32(act, weight_up, CONTRACT_LAST).astype(BF16)
    spread = dot_f32(
        placing, row_grad.reshape(n_expert, slots, width), (((1,), (1,)), ((0,), (0,)))
    ).astype(BF16)
    token_grad = lax.psum_scatter(
        spread.reshape(n_expert * tok_rows, width), "expert", scatter_dimension=0, tiled=True
    )
    up_grad = dot_f32(rows_in, act, CONTRACT_ROWS).astype(BF16)[None]
    down_grad = dot_f32(rows_cot, hidden, CONTRACT_ROWS).astype(BF16)[None]
    return token_grad, up_grad, down_grad


def solution(mesh):
    n_dp, n_expert = mesh.shape["dp"], mesh.shape["expert"]
    if n_dp == 2 and n_expert == NZ * NX * NC:
        body = grouped
    else:
        body = functools.partial(general, n_expert)
    return jax.shard_map(
        body,
        mesh=mesh,
        in_specs=(
            P("expert", "dp"),
            P("expert", "dp"),
            P("expert", None),
            P("expert", None),
            P(),
            P("expert", "dp", None),
            P("expert", "dp", None),
        ),
        out_specs=(P("expert", "dp"), P("expert", "dp", None), P("expert", "dp", None)),
        check_vma=False,
    )
```

```python
import functools

import jax
import jax.numpy as jnp
from jax import lax
from jax.experimental import pallas as pl
from jax.experimental.pallas import tpu as pltpu
from jax.sharding import PartitionSpec as P

F32 = jnp.float32
BF16 = jnp.bfloat16
CONTRACT_ROWS = (((0,), (0,)), ((), ()))
CONTRACT_LAST = (((1,), (1,)), ((), ()))

NO_COST = pl.CostEstimate(flops=0, bytes_accessed=0, transcendentals=0)

NZ, NX, NC = 4, 2, 2


def dot_f32(left, right, dims=(((1,), (0,)), ((), ()))):
    return lax.dot_general(left, right, dims, preferred_element_type=F32)


def swap_z(value, distance):
    step = distance * NX * NC
    return lax.ppermute(value, "expert", [(i, i ^ step) for i in range(NZ * NX * NC)])


def swap_x(value):
    return lax.ppermute(value, "expert", [(i, i ^ NC) for i in range(NZ * NX * NC)])


def swap_core(value):
    return lax.ppermute(value, "expert", [(i, i ^ 1) for i in range(NZ * NX * NC)])


def swap_dp(value):
    return lax.ppermute(value, "dp", [(0, 1), (1, 0)])


def tie(value, *earlier):
    return lax.optimization_barrier((value, earlier))[0]


def add(left, right):
    return (left.astype(F32) + right.astype(F32)).astype(BF16)


def placing_of(slot_row, slots):
    return slot_row == lax.broadcasted_iota(jnp.int32, (slots, slot_row.shape[1]), 0)


LANES = 128


def with_routing(tokens, expert_ids, gate_levels):
    half = LANES // 2
    room = ((0, 0), (0, half - expert_ids.shape[1]))
    parts = [tokens, jnp.pad(expert_ids, room).astype(BF16), jnp.pad(gate_levels, room).astype(BF16)]
    return jnp.concatenate(parts, axis=1)


def read_routing(meta, own, limit, top_count):
    tok_rows = meta.shape[0]
    ids = meta.astype(F32)
    levels = pltpu.roll(ids, LANES // 2, 1)
    choice = lax.broadcasted_iota(jnp.int32, ids.shape, 1) < top_count
    named = choice & (ids == own)
    ones = jnp.ones((8, LANES), BF16)
    match = dot_f32(ones, jnp.where(named, 1.0, 0.0).astype(BF16), CONTRACT_LAST)
    level = dot_f32(ones, jnp.where(named, levels, 0.0).astype(BF16), CONTRACT_LAST)
    total = dot_f32(ones, jnp.where(choice, levels, 0.0).astype(BF16), CONTRACT_LAST)
    square = (tok_rows, tok_rows)
    before = lax.broadcasted_iota(jnp.int32, square, 0) < lax.broadcasted_iota(jnp.int32, square, 1)
    rank = dot_f32(match.astype(BF16), jnp.where(before, 1.0, 0.0).astype(BF16))
    kept = (match > 0.5) & (rank < limit)
    return jnp.where(kept, rank, -1.0).astype(jnp.int32), level / total


def add_up(total, part_ref, product):
    step = pl.program_id(0)

    @pl.when(step == 0)
    def _():
        total[...] = product

    @pl.when(step > 0)
    def _():
        total[...] += product

    @pl.when(step == pl.num_programs(0) - 1)
    def _():
        part_ref[...] = total[...].astype(BF16)


def tokens_kernel(top_count, slots, own_ref, m0, m1, m2, m3, b0, b1, b2, b3, weight_ref, rows_ref, part_ref, slot_ref, gate_ref, total):
    @pl.when(pl.program_id(0) == 0)
    def _():
        own = own_ref[0].astype(F32)
        limit = own_ref[1].astype(F32)
        for index, meta in enumerate((m0, m1, m2, m3)):
            slot, gate = read_routing(meta[...], own, limit, top_count)
            slot_ref[index] = slot
            gate_ref[index] = gate

    for index, block in enumerate((b0, b1, b2, b3)):
        hit = placing_of(slot_ref[index, 0:1, :], slots)
        picked = dot_f32(jnp.where(hit, 1.0, 0.0).astype(BF16), block[...])
        rows_ref[index * slots : (index + 1) * slots, :] = picked.astype(BF16)
    add_up(total, part_ref, dot_f32(rows_ref[...], weight_ref[...]))


def cotangent_kernel(slots, slot_ref, gate_ref, b0, b1, b2, b3, weight_ref, rows_ref, part_ref, total):
    for index, block in enumerate((b0, b1, b2, b3)):
        hit = placing_of(slot_ref[index, 0:1, :], slots)
        picked = dot_f32(jnp.where(hit, 1.0, 0.0).astype(BF16), block[...])
        gate = jnp.sum(jnp.where(hit, gate_ref[index, 0:1, :], 0.0), axis=1, keepdims=True)
        rows_ref[index * slots : (index + 1) * slots, :] = (picked * gate).astype(BF16)
    add_up(total, part_ref, dot_f32(rows_ref[...], weight_ref[...]))


def front_specs(tok_rows, width, hidden, rows):
    tile = width // 2
    table = pl.BlockSpec((4, 8, tok_rows), lambda k: (0, 0, 0))
    blocks = [pl.BlockSpec((tok_rows, tile), lambda k: (0, k))] * 4
    weight = pl.BlockSpec((tile, hidden), lambda k: (k, 0))
    outs = [
        pl.BlockSpec((rows, tile), lambda k: (0, k)),
        pl.BlockSpec((rows, hidden), lambda k: (0, 0)),
    ]
    shapes = [jax.ShapeDtypeStruct((rows, width), BF16), jax.ShapeDtypeStruct((rows, hidden), BF16)]
    rest = dict(
        grid=(width // tile,),
        scratch_shapes=[pltpu.VMEM((rows, hidden), F32)],
        compiler_params=pltpu.CompilerParams(vmem_limit_bytes=24 * 1024 * 1024),
        cost_estimate=NO_COST,
    )
    return table, blocks, weight, outs, shapes, rest


def front_tokens(blocks, own, weight, slots, top_count):
    tok_rows = blocks[0].shape[0]
    width, hidden = weight.shape
    table, block_specs, weight_spec, outs, shapes, rest = front_specs(tok_rows, width, hidden, 4 * slots)
    meta = pl.BlockSpec((tok_rows, LANES), lambda k: (0, width // LANES))
    return pl.pallas_call(
        functools.partial(tokens_kernel, top_count, slots),
        in_specs=[pl.BlockSpec(memory_space=pltpu.SMEM)] + [meta] * 4 + block_specs + [weight_spec],
        out_specs=outs + [table, table],
        out_shape=shapes
        + [
            jax.ShapeDtypeStruct((4, 8, tok_rows), jnp.int32),
            jax.ShapeDtypeStruct((4, 8, tok_rows), F32),
        ],
        **rest,
    )(own, *blocks, *blocks, weight)


def front_cotangent(blocks, tables, weight, slots):
    tok_rows = blocks[0].shape[0]
    width, hidden = weight.shape
    table, block_specs, weight_spec, outs, shapes, rest = front_specs(tok_rows, width, hidden, 4 * slots)
    return pl.pallas_call(
        functools.partial(cotangent_kernel, slots),
        in_specs=[table, table] + block_specs + [weight_spec],
        out_specs=outs,
        out_shape=shapes,
        **rest,
    )(*tables, *blocks, weight)


def back_kernel(slots, slot_ref, pre_a, pre_b, cot_a, cot_b, weight_ref, act_ref, keep_ref, send_ref):
    @pl.when(pl.program_id(0) == 0)
    def _():
        preact = pre_a[...].astype(F32) + pre_b[...].astype(F32)
        hidden_cot = cot_a[...].astype(F32) + cot_b[...].astype(F32)
        sigmoid = jax.nn.sigmoid(preact)
        act_ref[...] = (hidden_cot * (sigmoid * (1.0 + preact * (1.0 - sigmoid)))).astype(BF16)

    back = dot_f32(act_ref[...], weight_ref[...], CONTRACT_LAST).astype(BF16)
    for index in range(4):
        hit = placing_of(slot_ref[index, 0:1, :], slots)
        placing = jnp.where(hit, 1.0, 0.0).astype(BF16)
        spread = dot_f32(placing, back[index * slots : (index + 1) * slots], CONTRACT_ROWS)
        out_ref = send_ref if index % 2 else keep_ref
        out_ref[index // 2] = spread.astype(BF16)


def back(slot_of, parts, weight, slots):
    tok_rows = slot_of.shape[2]
    width, hidden = weight.shape
    rows = 4 * slots
    tile = width // 2
    full = pl.BlockSpec((rows, hidden), lambda n: (0, 0))
    spread = pl.BlockSpec((2, tok_rows, tile), lambda n: (0, 0, n))
    return pl.pallas_call(
        functools.partial(back_kernel, slots),
        grid=(width // tile,),
        in_specs=[pl.BlockSpec((4, 8, tok_rows), lambda n: (0, 0, 0))]
        + [full] * 4
        + [pl.BlockSpec((tile, hidden), lambda n: (n, 0))],
        out_specs=[full, spread, spread],
        out_shape=[
            jax.ShapeDtypeStruct((rows, hidden), BF16),
            jax.ShapeDtypeStruct((2, tok_rows, width), BF16),
            jax.ShapeDtypeStruct((2, tok_rows, width), BF16),
        ],
        compiler_params=pltpu.CompilerParams(vmem_limit_bytes=32 * 1024 * 1024),
        cost_estimate=NO_COST,
    )(slot_of, *parts, weight)


def up_grad_kernel(*refs):
    count = (len(refs) - 1) // 2
    total = None
    for left, right in zip(refs[:count], refs[count:-1]):
        term = dot_f32(left[...], right[...], CONTRACT_ROWS)
        total = term if total is None else total + term
    refs[-1][...] = total.astype(BF16)


def down_grad_kernel(*refs):
    count = (len(refs) - 2) // 3
    out_ref, hidden_ref = refs[-2:]

    @pl.when(pl.program_id(0) == 0)
    def _():
        for index, (first, second) in enumerate(zip(refs[count : 2 * count], refs[2 * count : -2])):
            preact = first[...].astype(F32) + second[...].astype(F32)
            hidden_ref[index] = (preact * jax.nn.sigmoid(preact)).astype(BF16)

    total = None
    for index, left in enumerate(refs[:count]):
        term = dot_f32(left[...], hidden_ref[index], CONTRACT_ROWS)
        total = term if total is None else total + term
    out_ref[...] = total.astype(BF16)


def weight_grad(kernel, lefts, rights, scratch_shapes):
    rows, width = lefts[0].shape
    hidden = rights[0].shape[1]
    count = len(lefts)
    tile = 256
    return pl.pallas_call(
        kernel,
        grid=(width // tile,),
        in_specs=[pl.BlockSpec((rows, tile), lambda n: (0, n))] * count
        + [pl.BlockSpec((rows, hidden), lambda n: (0, 0))] * len(rights),
        out_specs=pl.BlockSpec((tile, hidden), lambda n: (n, 0)),
        out_shape=jax.ShapeDtypeStruct((width, hidden), BF16),
        scratch_shapes=scratch_shapes,
        compiler_params=pltpu.CompilerParams(vmem_limit_bytes=32 * 1024 * 1024),
        cost_estimate=NO_COST,
    )(*lefts, *rights)


def slots_and_gates(routing, own, limit, top_count):
    ids = routing[:, :, :top_count]
    levels = routing[:, :, top_count:].astype(F32)
    tok_rows = ids.shape[1]
    named = ids == own
    match = jnp.any(named, axis=2)
    gates = jnp.sum(jnp.where(named, levels, 0.0), axis=2) / jnp.sum(levels, axis=2)
    before = jnp.arange(tok_rows)[:, None] < jnp.arange(tok_rows)[None, :]
    rank = dot_f32(match.astype(BF16), before.astype(BF16)).astype(jnp.int32)
    return jnp.where(match & (rank < limit), rank, -1), gates


def grouped(tokens, cotangent, expert_ids, gate_levels, capacity, up_weight, down_weight):
    top_count = expert_ids.shape[1]
    slots = tokens.shape[0] * top_count // capacity.shape[0]
    own = lax.axis_index("expert")
    who = jnp.stack([own.astype(jnp.int32), capacity[own]])
    weight_up, weight_down = up_weight[0], down_weight[0]

    rows_in, rows_cot, tables, pre, cot = ([None] * NZ for _ in range(5))

    def first(s, mine, mine_core, other):
        blocks = (mine, mine_core, other, swap_core(other))
        rows_in[s], part, slot, gate = front_tokens(blocks, who, weight_up, slots, top_count)
        tables[s] = (slot, gate)
        pre[s] = (part, swap_dp(part))

    def second(s, mine, mine_core, other):
        blocks = (mine, mine_core, other, swap_core(other))
        rows_cot[s], part = front_cotangent(blocks, tables[s], weight_down, slots)
        cot[s] = (part, swap_dp(part))

    act, chip = [None] * NZ, [None] * NZ

    def last(s, *earlier):
        parts = tie(pre[s] + cot[s], *earlier)
        act[s], keep, send = back(tables[s][0], parts, weight_up, slots)
        chip[s] = add(keep, swap_core(send))

    z = own // (NX * NC)
    columns = [[(k * NX + x) * NC + c for k in range(NZ)] for x in range(NX) for c in range(NC)]

    def along_z(value):
        return lax.all_gather(value, "expert", axis_index_groups=columns)

    def at_distance(column, distance):
        return lax.dynamic_index_in_dim(column, z ^ distance, 0, keepdims=False)

    tok = with_routing(tokens, expert_ids, gate_levels)
    tok_column = along_z(tok)
    cot_column = along_z(cotangent)
    x_own = swap_x(tok)
    tok_core = swap_core(tok)
    cot_own = tie(cotangent, x_own)
    x_cot = swap_x(cot_own)
    cot_core = swap_core(cot_own)
    first(0, tok, tok_core, x_own)
    second(0, cot_own, cot_core, tie(x_cot, pre[0][1]))

    near = at_distance(tok_column, 1)
    x_near = swap_x(tie(near, x_cot, cot[0][0]))
    two = at_distance(tok_column, 2)
    far = at_distance(tok_column, 3)
    x_two = swap_x(tie(two, x_near))
    first(1, near, swap_core(near), x_near)
    x_far = swap_x(tie(far, x_two, pre[1][0], cot[0][1]))
    first(2, two, swap_core(two), x_two)
    last(0)

    cot_far = tie(at_distance(cot_column, 3), x_far, pre[2][0], pre[1][1])
    x_next = swap_x(cot_far)
    first(3, far, swap_core(far), x_far)
    cot_two = tie(at_distance(cot_column, 2), x_next, pre[3][0], pre[2][1])
    x_then = swap_x(cot_two)
    second(3, cot_far, swap_core(cot_far), x_next)
    cot_near = tie(at_distance(cot_column, 1), x_then, cot[3][0], pre[3][1])
    x_next = swap_x(cot_near)
    second(2, cot_two, swap_core(cot_two), x_then)
    x_own = swap_x(tie(chip[0][1], x_next, cot[2][0], cot[3][1]))
    second(1, cot_near, swap_core(cot_near), x_next)
    last(3)
    x_far = swap_x(tie(chip[3][1], cot[1][0]))
    last(2, cot[1][0])
    x_two = swap_x(tie(chip[2][1], x_far))
    hop_far = swap_z(add(chip[3][0], x_far), 3)
    down_grad = weight_grad(
        down_grad_kernel,
        rows_cot,
        [p[0] for p in pre] + [p[1] for p in pre],
        [pltpu.VMEM((NZ,) + pre[0][0].shape, BF16)],
    )
    last(1, down_grad)
    x_near = swap_x(tie(chip[1][1], x_two))
    hop_two = swap_z(add(chip[2][0], x_two), 2)
    hop_near = swap_z(add(chip[1][0], x_near), 1)
    up_grad = weight_grad(up_grad_kernel, rows_in, act, [])
    own_sum = chip[0][0].astype(F32) + x_own.astype(F32)
    token_grad = (
        own_sum + hop_near.astype(F32) + hop_two.astype(F32) + hop_far.astype(F32)
    ).astype(BF16)
    return token_grad, up_grad[None], down_grad[None]


def general(n_expert, tokens, cotangent, expert_ids, gate_levels, capacity, up_weight, down_weight):
    tok_rows, width = tokens.shape
    top_count = expert_ids.shape[1]
    slots = tok_rows * top_count // capacity.shape[0]
    row_count = n_expert * slots
    own = lax.axis_index("expert")
    weight_up, weight_down = up_weight[0], down_weight[0]

    routing = lax.all_gather(
        jnp.concatenate([expert_ids, gate_levels], axis=1), "expert", axis=0, tiled=False
    )
    tok_all = lax.all_gather(tokens, "expert", axis=0, tiled=False)
    cot_all = lax.all_gather(cotangent, "expert", axis=0, tiled=False)
    slot_of, gates = slots_and_gates(routing, own, capacity[own], top_count)
    placing = slot_of[:, None, :] == jnp.arange(slots, dtype=jnp.int32)[None, :, None]
    slot_gate = jnp.sum(jnp.where(placing, gates[:, None, :], 0.0), axis=2)
    placing = placing.astype(BF16)
    pick = (((2,), (1,)), ((0,), (0,)))
    rows_in = dot_f32(placing, tok_all, pick).astype(BF16).reshape(row_count, width)
    rows_cot = (slot_gate[:, :, None] * dot_f32(placing, cot_all, pick)).astype(BF16)
    rows_cot = rows_cot.reshape(row_count, width)
    preact = lax.psum(dot_f32(rows_in, weight_up).astype(BF16).astype(F32), "dp")
    hidden_cot = lax.psum(dot_f32(rows_cot, weight_down).astype(BF16).astype(F32), "dp")
    sigmoid = jax.nn.sigmoid(preact)
    hidden = (preact * sigmoid).astype(BF16)
    act = (hidden_cot * (sigmoid * (1.0 + preact * (1.0 - sigmoid)))).astype(BF16)
    row_grad = dot_f32(act, weight_up, CONTRACT_LAST).astype(BF16)
    spread = dot_f32(
        placing, row_grad.reshape(n_expert, slots, width), (((1,), (1,)), ((0,), (0,)))
    ).astype(BF16)
    token_grad = lax.psum_scatter(
        spread.reshape(n_expert * tok_rows, width), "expert", scatter_dimension=0, tiled=True
    )
    up_grad = dot_f32(rows_in, act, CONTRACT_ROWS).astype(BF16)[None]
    down_grad = dot_f32(rows_cot, hidden, CONTRACT_ROWS).astype(BF16)[None]
    return token_grad, up_grad, down_grad


def solution(mesh):
    n_dp, n_expert = mesh.shape["dp"], mesh.shape["expert"]
    if n_dp == 2 and n_expert == NZ * NX * NC:
        body = grouped
    else:
        body = functools.partial(general, n_expert)
    return jax.shard_map(
        body,
        mesh=mesh,
        in_specs=(
            P("expert", "dp"),
            P("expert", "dp"),
            P("expert", None),
            P("expert", None),
            P(),
            P("expert", "dp", None),
            P("expert", "dp", None),
        ),
        out_specs=(P("expert", "dp"), P("expert", "dp", None), P("expert", "dp", None)),
        check_vma=False,
    )
```

```python
import functools

import jax
import jax.numpy as jnp
from jax import lax
from jax.experimental import pallas as pl
from jax.experimental.pallas import tpu as pltpu
from jax.sharding import PartitionSpec as P

F32 = jnp.float32
BF16 = jnp.bfloat16
CONTRACT_ROWS = (((0,), (0,)), ((), ()))
CONTRACT_LAST = (((1,), (1,)), ((), ()))

NO_COST = pl.CostEstimate(flops=0, bytes_accessed=0, transcendentals=0)

NZ, NX, NC = 4, 2, 2


def dot_f32(left, right, dims=(((1,), (0,)), ((), ()))):
    return lax.dot_general(left, right, dims, preferred_element_type=F32)


def along_z(value, pairs):
    perm = [
        ((a * NX + x) * NC + c, (b * NX + x) * NC + c)
        for a, b in pairs
        for x in range(NX)
        for c in range(NC)
    ]
    return lax.ppermute(value, "expert", perm)


def swap_x(value):
    return lax.ppermute(value, "expert", [(i, i ^ NC) for i in range(NZ * NX * NC)])


def swap_core(value):
    return lax.ppermute(value, "expert", [(i, i ^ 1) for i in range(NZ * NX * NC)])


def swap_dp(value):
    return lax.ppermute(value, "dp", [(0, 1), (1, 0)])


NEIGHBOUR = ((0, 1), (1, 0), (2, 3), (3, 2))
MIDDLE = ((1, 2), (2, 1))
OUTWARD = ((1, 0), (2, 3))
TWO_INWARD = ((0, 2), (3, 1))
TWO_OUTWARD = ((1, 3), (2, 0))
THREE = ((0, 3), (3, 0))


def tie(value, *earlier):
    return lax.optimization_barrier((value, earlier))[0]


def add(left, right):
    return (left.astype(F32) + right.astype(F32)).astype(BF16)


def placing_of(slot_row, slots):
    return slot_row == lax.broadcasted_iota(jnp.int32, (slots, slot_row.shape[1]), 0)


LANES = 128


def joined(tokens, cotangent, expert_ids, gate_levels):
    room = ((0, 0), (0, LANES // 2 - expert_ids.shape[1]))
    tables = [jnp.pad(table.astype(BF16), room) for table in (expert_ids, gate_levels)]
    return jnp.concatenate([tokens, cotangent] + tables, axis=1)


def read_routing(meta, own, limit, top_count):
    tok_rows = meta.shape[0]
    ids = meta.astype(F32)
    levels = pltpu.roll(ids, LANES // 2, 1)
    choice = lax.broadcasted_iota(jnp.int32, ids.shape, 1) < top_count
    named = choice & (ids == own)
    ones = jnp.ones((8, LANES), BF16)
    match = dot_f32(ones, jnp.where(named, 1.0, 0.0).astype(BF16), CONTRACT_LAST)
    level = dot_f32(ones, jnp.where(named, levels, 0.0).astype(BF16), CONTRACT_LAST)
    total = dot_f32(ones, jnp.where(choice, levels, 0.0).astype(BF16), CONTRACT_LAST)
    square = (tok_rows, tok_rows)
    before = lax.broadcasted_iota(jnp.int32, square, 0) < lax.broadcasted_iota(jnp.int32, square, 1)
    rank = dot_f32(match.astype(BF16), jnp.where(before, 1.0, 0.0).astype(BF16))
    kept = (match > 0.5) & (rank < limit)
    return jnp.where(kept, rank, -1.0).astype(jnp.int32), level / total


def front_kernel(top_count, slots, own_ref, *refs):
    metas, tok_blocks, cot_blocks = refs[:4], refs[4:8], refs[8:12]
    up_ref, down_ref, rows_ref, rows_cot_ref, part_ref, slot_ref, gates, total = refs[12:]
    step, hidden = pl.program_id(0), up_ref.shape[1]

    @pl.when(step == 0)
    def _():
        own = own_ref[0].astype(F32)
        limit = own_ref[1].astype(F32)
        for index, meta in enumerate(metas):
            slot, gate = read_routing(meta[...], own, limit, top_count)
            slot_ref[index] = slot
            gates[index] = gate

    for index in range(4):
        hit = placing_of(slot_ref[index, 0:1, :], slots)
        placing = jnp.where(hit, 1.0, 0.0).astype(BF16)
        gate = jnp.sum(jnp.where(hit, gates[index, 0:1, :], 0.0), axis=1, keepdims=True)
        here = slice(index * slots, (index + 1) * slots)
        rows_ref[here, :] = dot_f32(placing, tok_blocks[index][...]).astype(BF16)
        rows_cot_ref[here, :] = (gate * dot_f32(placing, cot_blocks[index][...])).astype(BF16)
    products = (dot_f32(rows_ref[...], up_ref[...]), dot_f32(rows_cot_ref[...], down_ref[...]))

    @pl.when(step == 0)
    def _():
        for half, product in enumerate(products):
            total[half] = product

    @pl.when(step > 0)
    def _():
        for half, product in enumerate(products):
            total[half] += product

    @pl.when(step == pl.num_programs(0) - 1)
    def _():
        for half in range(2):
            part_ref[:, half * hidden : (half + 1) * hidden] = total[half].astype(BF16)


def front(blocks, own, weight_up, weight_down, slots, top_count):
    tok_rows = blocks[0].shape[0]
    width, hidden = weight_up.shape
    rows = 4 * slots
    tile = width // 2
    weight = pl.BlockSpec((tile, hidden), lambda k: (k, 0))
    picked = pl.BlockSpec((rows, tile), lambda k: (0, k))
    return pl.pallas_call(
        functools.partial(front_kernel, top_count, slots),
        grid=(width // tile,),
        in_specs=[pl.BlockSpec(memory_space=pltpu.SMEM)]
        + [pl.BlockSpec((tok_rows, LANES), lambda k: (0, 2 * width // LANES))] * 4
        + [pl.BlockSpec((tok_rows, tile), lambda k: (0, k))] * 4
        + [pl.BlockSpec((tok_rows, tile), lambda k: (0, width // tile + k))] * 4
        + [weight, weight],
        out_specs=[
            picked,
            picked,
            pl.BlockSpec((rows, 2 * hidden), lambda k: (0, 0)),
            pl.BlockSpec((4, 8, tok_rows), lambda k: (0, 0, 0)),
        ],
        out_shape=[
            jax.ShapeDtypeStruct((rows, width), BF16),
            jax.ShapeDtypeStruct((rows, width), BF16),
            jax.ShapeDtypeStruct((rows, 2 * hidden), BF16),
            jax.ShapeDtypeStruct((4, 8, tok_rows), jnp.int32),
        ],
        scratch_shapes=[
            pltpu.VMEM((4, 8, tok_rows), F32),
            pltpu.VMEM((2, rows, hidden), F32),
        ],
        compiler_params=pltpu.CompilerParams(vmem_limit_bytes=32 * 1024 * 1024),
        cost_estimate=NO_COST,
    )(own, *blocks, *blocks, *blocks, weight_up, weight_down)


def back_kernel(slots, slot_ref, part_a, part_b, weight_ref, act_ref, keep_ref, send_ref):
    @pl.when(pl.program_id(0) == 0)
    def _():
        hidden = act_ref.shape[1]
        preact = part_a[:, :hidden].astype(F32) + part_b[:, :hidden].astype(F32)
        hidden_cot = part_a[:, hidden:].astype(F32) + part_b[:, hidden:].astype(F32)
        sigmoid = jax.nn.sigmoid(preact)
        act_ref[...] = (hidden_cot * (sigmoid * (1.0 + preact * (1.0 - sigmoid)))).astype(BF16)

    back = dot_f32(act_ref[...], weight_ref[...], CONTRACT_LAST).astype(BF16)
    for index in range(4):
        hit = placing_of(slot_ref[index, 0:1, :], slots)
        placing = jnp.where(hit, 1.0, 0.0).astype(BF16)
        spread = dot_f32(placing, back[index * slots : (index + 1) * slots], CONTRACT_ROWS)
        out_ref = send_ref if index % 2 else keep_ref
        out_ref[index // 2] = spread.astype(BF16)


def back(slot_of, parts, weight, slots):
    tok_rows = slot_of.shape[2]
    width, hidden = weight.shape
    rows = 4 * slots
    tile = width // 2
    full = pl.BlockSpec((rows, hidden), lambda n: (0, 0))
    spread = pl.BlockSpec((2, tok_rows, tile), lambda n: (0, 0, n))
    return pl.pallas_call(
        functools.partial(back_kernel, slots),
        grid=(width // tile,),
        in_specs=[pl.BlockSpec((4, 8, tok_rows), lambda n: (0, 0, 0))]
        + [pl.BlockSpec((rows, 2 * hidden), lambda n: (0, 0))] * 2
        + [pl.BlockSpec((tile, hidden), lambda n: (n, 0))],
        out_specs=[full, spread, spread],
        out_shape=[
            jax.ShapeDtypeStruct((rows, hidden), BF16),
            jax.ShapeDtypeStruct((2, tok_rows, width), BF16),
            jax.ShapeDtypeStruct((2, tok_rows, width), BF16),
        ],
        compiler_params=pltpu.CompilerParams(vmem_limit_bytes=32 * 1024 * 1024),
        cost_estimate=NO_COST,
    )(slot_of, *parts, weight)


def up_grad_kernel(*refs):
    count = (len(refs) - 1) // 2
    total = None
    for left, right in zip(refs[:count], refs[count:-1]):
        term = dot_f32(left[...], right[...], CONTRACT_ROWS)
        total = term if total is None else total + term
    refs[-1][...] = total.astype(BF16)


def down_grad_kernel(*refs):
    count = (len(refs) - 2) // 3
    out_ref, hidden_ref = refs[-2:]

    @pl.when(pl.program_id(0) == 0)
    def _():
        for index, (first, second) in enumerate(zip(refs[count : 2 * count], refs[2 * count : -2])):
            preact = first[...].astype(F32) + second[...].astype(F32)
            hidden_ref[index] = (preact * jax.nn.sigmoid(preact)).astype(BF16)

    total = None
    for index, left in enumerate(refs[:count]):
        term = dot_f32(left[...], hidden_ref[index], CONTRACT_ROWS)
        total = term if total is None else total + term
    out_ref[...] = total.astype(BF16)


def weight_grad(kernel, hidden, lefts, rights, scratch_shapes):
    rows, width = lefts[0].shape
    count = len(lefts)
    tile = 256
    return pl.pallas_call(
        kernel,
        grid=(width // tile,),
        in_specs=[pl.BlockSpec((rows, tile), lambda n: (0, n))] * count
        + [pl.BlockSpec((rows, hidden), lambda n: (0, 0))] * len(rights),
        out_specs=pl.BlockSpec((tile, hidden), lambda n: (n, 0)),
        out_shape=jax.ShapeDtypeStruct((width, hidden), BF16),
        scratch_shapes=scratch_shapes,
        compiler_params=pltpu.CompilerParams(vmem_limit_bytes=32 * 1024 * 1024),
        cost_estimate=NO_COST,
    )(*lefts, *rights)


def slots_and_gates(routing, own, limit, top_count):
    ids = routing[:, :, :top_count]
    levels = routing[:, :, top_count:].astype(F32)
    tok_rows = ids.shape[1]
    named = ids == own
    match = jnp.any(named, axis=2)
    gates = jnp.sum(jnp.where(named, levels, 0.0), axis=2) / jnp.sum(levels, axis=2)
    before = jnp.arange(tok_rows)[:, None] < jnp.arange(tok_rows)[None, :]
    rank = dot_f32(match.astype(BF16), before.astype(BF16)).astype(jnp.int32)
    return jnp.where(match & (rank < limit), rank, -1), gates


def grouped(tokens, cotangent, expert_ids, gate_levels, capacity, up_weight, down_weight):
    top_count = expert_ids.shape[1]
    slots = tokens.shape[0] * top_count // capacity.shape[0]
    own = lax.axis_index("expert")
    z = own // (NX * NC)
    inner = (z > 0) & (z < NZ - 1)
    who = jnp.stack([own.astype(jnp.int32), capacity[own]])
    weight_up, weight_down = up_weight[0], down_weight[0]

    hidden_units = weight_up.shape[1]

    rows_in, rows_cot, slot_of, parts, act, chip = ([None] * NZ for _ in range(6))

    def forth(s, *blocks):
        rows_in[s], rows_cot[s], part, slot_of[s] = front(
            blocks, who, weight_up, weight_down, slots, top_count
        )
        parts[s] = (part, swap_dp(part))

    def back_again(s, *earlier):
        pair = tie(parts[s], *earlier)
        act[s], keep, send = back(slot_of[s], pair, weight_up, slots)
        chip[s] = add(keep, swap_core(send))

    block = joined(tokens, cotangent, expert_ids, gate_levels)
    x_own = swap_x(block)
    near = along_z(block, NEIGHBOUR)
    two_in = along_z(block, MIDDLE)
    own_core = swap_core(block)

    near, two_in = tie((near, two_in), x_own)
    x_near = swap_x(near)
    far_in = along_z(near, MIDDLE)
    two_out = along_z(two_in, OUTWARD)
    near_core = swap_core(near)
    forth(0, block, own_core, x_own, swap_core(x_own))

    two, far_in = tie((jnp.where(inner, two_in, two_out), far_in), x_near, parts[0][0])
    x_two = swap_x(two)
    far_out = along_z(far_in, OUTWARD)
    two_core = swap_core(two)
    forth(1, near, near_core, x_near, swap_core(x_near))

    far = tie(jnp.where(inner, far_in, far_out), x_two, parts[1][0], parts[0][1])
    x_far = swap_x(far)
    far_core = swap_core(far)
    forth(2, two, two_core, x_two, swap_core(x_two))
    back_again(0)

    own_send = tie(chip[0][1], x_far, parts[2][0], parts[1][1])
    back_own = swap_x(own_send)
    forth(3, far, far_core, x_far, swap_core(x_far))
    back_again(1)

    near_send = tie(chip[1][1], back_own, parts[3][0])
    back_near = swap_x(near_send)
    back_again(2)
    near_sum = add(chip[1][0], back_near)
    hop_near = along_z(near_sum, NEIGHBOUR)

    two_send = tie(chip[2][1], back_near)
    back_two = swap_x(two_send)
    two_sum = add(chip[2][0], back_two)
    hops_two = (along_z(two_sum, MIDDLE), along_z(two_sum, TWO_INWARD))
    back_again(3, near_sum)
    down_grad = weight_grad(
        down_grad_kernel,
        hidden_units,
        tie(rows_cot, chip[3]),
        [p[0] for p in parts] + [p[1] for p in parts],
        [pltpu.VMEM((NZ, parts[0][0].shape[0], hidden_units), BF16)],
    )

    far_send = tie(chip[3][1], back_two)
    back_far = swap_x(far_send)
    far_sum = tie(add(chip[3][0], back_far), *hops_two)
    hops_far = (along_z(far_sum, THREE), along_z(far_sum, TWO_OUTWARD))
    up_grad = weight_grad(up_grad_kernel, hidden_units, rows_in, act, [])
    own_sum = chip[0][0].astype(F32) + back_own.astype(F32)
    for hop in (hop_near, *hops_two, *hops_far):
        own_sum = own_sum + hop.astype(F32)
    token_grad = own_sum.astype(BF16)
    return token_grad, up_grad[None], down_grad[None]


def general(n_expert, tokens, cotangent, expert_ids, gate_levels, capacity, up_weight, down_weight):
    tok_rows, width = tokens.shape
    top_count = expert_ids.shape[1]
    slots = tok_rows * top_count // capacity.shape[0]
    row_count = n_expert * slots
    own = lax.axis_index("expert")
    weight_up, weight_down = up_weight[0], down_weight[0]

    routing = lax.all_gather(
        jnp.concatenate([expert_ids, gate_levels], axis=1), "expert", axis=0, tiled=False
    )
    tok_all = lax.all_gather(tokens, "expert", axis=0, tiled=False)
    cot_all = lax.all_gather(cotangent, "expert", axis=0, tiled=False)
    slot_of, gates = slots_and_gates(routing, own, capacity[own], top_count)
    placing = slot_of[:, None, :] == jnp.arange(slots, dtype=jnp.int32)[None, :, None]
    slot_gate = jnp.sum(jnp.where(placing, gates[:, None, :], 0.0), axis=2)
    placing = placing.astype(BF16)
    pick = (((2,), (1,)), ((0,), (0,)))
    rows_in = dot_f32(placing, tok_all, pick).astype(BF16).reshape(row_count, width)
    rows_cot = (slot_gate[:, :, None] * dot_f32(placing, cot_all, pick)).astype(BF16)
    rows_cot = rows_cot.reshape(row_count, width)
    preact = lax.psum(dot_f32(rows_in, weight_up).astype(BF16).astype(F32), "dp")
    hidden_cot = lax.psum(dot_f32(rows_cot, weight_down).astype(BF16).astype(F32), "dp")
    sigmoid = jax.nn.sigmoid(preact)
    hidden = (preact * sigmoid).astype(BF16)
    act = (hidden_cot * (sigmoid * (1.0 + preact * (1.0 - sigmoid)))).astype(BF16)
    row_grad = dot_f32(act, weight_up, CONTRACT_LAST).astype(BF16)
    spread = dot_f32(
        placing, row_grad.reshape(n_expert, slots, width), (((1,), (1,)), ((0,), (0,)))
    ).astype(BF16)
    token_grad = lax.psum_scatter(
        spread.reshape(n_expert * tok_rows, width), "expert", scatter_dimension=0, tiled=True
    )
    up_grad = dot_f32(rows_in, act, CONTRACT_ROWS).astype(BF16)[None]
    down_grad = dot_f32(rows_cot, hidden, CONTRACT_ROWS).astype(BF16)[None]
    return token_grad, up_grad, down_grad


def solution(mesh):
    n_dp, n_expert = mesh.shape["dp"], mesh.shape["expert"]
    if n_dp == 2 and n_expert == NZ * NX * NC:
        body = grouped
    else:
        body = functools.partial(general, n_expert)
    return jax.shard_map(
        body,
        mesh=mesh,
        in_specs=(
            P("expert", "dp"),
            P("expert", "dp"),
            P("expert", None),
            P("expert", None),
            P(),
            P("expert", "dp", None),
            P("expert", "dp", None),
        ),
        out_specs=(P("expert", "dp"), P("expert", "dp", None), P("expert", "dp", None)),
        check_vma=False,
    )
```

```python
import functools

import jax
import jax.numpy as jnp
from jax import lax
from jax.experimental import pallas as pl
from jax.experimental.pallas import tpu as pltpu
from jax.sharding import PartitionSpec as P

F32 = jnp.float32
BF16 = jnp.bfloat16
CONTRACT_ROWS = (((0,), (0,)), ((), ()))
CONTRACT_LAST = (((1,), (1,)), ((), ()))

NO_COST = pl.CostEstimate(flops=0, bytes_accessed=0, transcendentals=0)

NZ, NX, NC = 4, 2, 2


def dot_f32(left, right, dims=(((1,), (0,)), ((), ()))):
    return lax.dot_general(left, right, dims, preferred_element_type=F32)


def along_z(value, pairs):
    perm = [
        ((a * NX + x) * NC + c, (b * NX + x) * NC + c)
        for a, b in pairs
        for x in range(NX)
        for c in range(NC)
    ]
    return lax.ppermute(value, "expert", perm)


def swap_z(value, distance):
    step = distance * NX * NC
    return lax.ppermute(value, "expert", [(i, i ^ step) for i in range(NZ * NX * NC)])


def swap_x(value):
    return lax.ppermute(value, "expert", [(i, i ^ NC) for i in range(NZ * NX * NC)])


def swap_core(value):
    return lax.ppermute(value, "expert", [(i, i ^ 1) for i in range(NZ * NX * NC)])


def swap_dp(value):
    return lax.ppermute(value, "dp", [(0, 1), (1, 0)])


NEIGHBOUR = ((0, 1), (1, 0), (2, 3), (3, 2))
MIDDLE = ((1, 2), (2, 1))
OUTWARD = ((1, 0), (2, 3))


def tie(value, *earlier):
    return lax.optimization_barrier((value, earlier))[0]


def add(left, right):
    return (left.astype(F32) + right.astype(F32)).astype(BF16)


def placing_of(slot_row, slots):
    return slot_row == lax.broadcasted_iota(jnp.int32, (slots, slot_row.shape[1]), 0)


LANES = 128


def joined(tokens, cotangent, expert_ids, gate_levels):
    gap = LANES // 2 - expert_ids.shape[1]
    table = jnp.pad(expert_ids, ((0, 0), (0, gap + LANES // 2)))
    table = table + jnp.pad(gate_levels, ((0, 0), (LANES // 2, gap)))
    return jnp.concatenate([tokens, cotangent, table.astype(BF16)], axis=1)


def read_routing(meta, own, limit, top_count):
    tok_rows = meta.shape[0]
    ids = meta.astype(F32)
    levels = pltpu.roll(ids, LANES // 2, 1)
    choice = lax.broadcasted_iota(jnp.int32, ids.shape, 1) < top_count
    named = choice & (ids == own)
    ones = jnp.ones((8, LANES), BF16)
    match = dot_f32(ones, jnp.where(named, 1.0, 0.0).astype(BF16), CONTRACT_LAST)
    level = dot_f32(ones, jnp.where(named, levels, 0.0).astype(BF16), CONTRACT_LAST)
    total = dot_f32(ones, jnp.where(choice, levels, 0.0).astype(BF16), CONTRACT_LAST)
    square = (tok_rows, tok_rows)
    before = lax.broadcasted_iota(jnp.int32, square, 0) < lax.broadcasted_iota(jnp.int32, square, 1)
    rank = dot_f32(match.astype(BF16), jnp.where(before, 1.0, 0.0).astype(BF16))
    kept = (match > 0.5) & (rank < limit)
    return jnp.where(kept, rank, -1.0).astype(jnp.int32), level / total


def front_kernel(top_count, slots, own_ref, capacity_ref, *refs):
    metas, tok_blocks, cot_blocks = refs[:4], refs[4:8], refs[8:12]
    up_ref, down_ref, rows_ref, rows_cot_ref, part_ref, slot_ref, gates, total = refs[12:]
    step, hidden = pl.program_id(0), up_ref.shape[1]

    @pl.when(step == 0)
    def _():
        own = own_ref[0].astype(F32)
        limit = capacity_ref[own_ref[0]].astype(F32)
        for index, meta in enumerate(metas):
            slot, gate = read_routing(meta[...], own, limit, top_count)
            slot_ref[index] = slot
            gates[index] = gate

    for index in range(4):
        hit = placing_of(slot_ref[index, 0:1, :], slots)
        placing = jnp.where(hit, 1.0, 0.0).astype(BF16)
        gate = jnp.sum(jnp.where(hit, gates[index, 0:1, :], 0.0), axis=1, keepdims=True)
        here = slice(index * slots, (index + 1) * slots)
        rows_ref[here, :] = dot_f32(placing, tok_blocks[index][...]).astype(BF16)
        rows_cot_ref[here, :] = (gate * dot_f32(placing, cot_blocks[index][...])).astype(BF16)
    products = (dot_f32(rows_ref[...], up_ref[...]), dot_f32(rows_cot_ref[...], down_ref[...]))

    @pl.when(step == 0)
    def _():
        for half, product in enumerate(products):
            total[half] = product

    @pl.when(step > 0)
    def _():
        for half, product in enumerate(products):
            total[half] += product

    @pl.when(step == pl.num_programs(0) - 1)
    def _():
        for half in range(2):
            part_ref[:, half * hidden : (half + 1) * hidden] = total[half].astype(BF16)


def front(blocks, own, capacity, weight_up, weight_down, slots, top_count):
    tok_rows = blocks[0].shape[0]
    width, hidden = weight_up.shape
    rows = 4 * slots
    tile = width // 2
    weight = pl.BlockSpec((tile, hidden), lambda k: (k, 0))
    picked = pl.BlockSpec((rows, tile), lambda k: (0, k))
    return pl.pallas_call(
        functools.partial(front_kernel, top_count, slots),
        grid=(width // tile,),
        in_specs=[pl.BlockSpec(memory_space=pltpu.SMEM)] * 2
        + [pl.BlockSpec((tok_rows, LANES), lambda k: (0, 2 * width // LANES))] * 4
        + [pl.BlockSpec((tok_rows, tile), lambda k: (0, k))] * 4
        + [pl.BlockSpec((tok_rows, tile), lambda k: (0, width // tile + k))] * 4
        + [weight, weight],
        out_specs=[
            picked,
            picked,
            pl.BlockSpec((rows, 2 * hidden), lambda k: (0, 0)),
            pl.BlockSpec((4, 8, tok_rows), lambda k: (0, 0, 0)),
        ],
        out_shape=[
            jax.ShapeDtypeStruct((rows, width), BF16),
            jax.ShapeDtypeStruct((rows, width), BF16),
            jax.ShapeDtypeStruct((rows, 2 * hidden), BF16),
            jax.ShapeDtypeStruct((4, 8, tok_rows), jnp.int32),
        ],
        scratch_shapes=[
            pltpu.VMEM((4, 8, tok_rows), F32),
            pltpu.VMEM((2, rows, hidden), F32),
        ],
        compiler_params=pltpu.CompilerParams(vmem_limit_bytes=32 * 1024 * 1024),
        cost_estimate=NO_COST,
    )(own, capacity, *blocks, *blocks, *blocks, weight_up, weight_down)


def back_kernel(slots, slot_ref, part_a, part_b, weight_ref, act_ref, keep_ref, send_ref):
    @pl.when(pl.program_id(0) == 0)
    def _():
        hidden = act_ref.shape[1]
        preact = part_a[:, :hidden].astype(F32) + part_b[:, :hidden].astype(F32)
        hidden_cot = part_a[:, hidden:].astype(F32) + part_b[:, hidden:].astype(F32)
        sigmoid = jax.nn.sigmoid(preact)
        act_ref[...] = (hidden_cot * (sigmoid * (1.0 + preact * (1.0 - sigmoid)))).astype(BF16)

    back = dot_f32(act_ref[...], weight_ref[...], CONTRACT_LAST).astype(BF16)
    for index in range(4):
        hit = placing_of(slot_ref[index, 0:1, :], slots)
        placing = jnp.where(hit, 1.0, 0.0).astype(BF16)
        spread = dot_f32(placing, back[index * slots : (index + 1) * slots], CONTRACT_ROWS)
        out_ref = send_ref if index % 2 else keep_ref
        out_ref[index // 2] = spread.astype(BF16)


def back(slot_of, parts, weight, slots):
    tok_rows = slot_of.shape[2]
    width, hidden = weight.shape
    rows = 4 * slots
    tile = width // 2
    full = pl.BlockSpec((rows, hidden), lambda n: (0, 0))
    spread = pl.BlockSpec((2, tok_rows, tile), lambda n: (0, 0, n))
    return pl.pallas_call(
        functools.partial(back_kernel, slots),
        grid=(width // tile,),
        in_specs=[pl.BlockSpec((4, 8, tok_rows), lambda n: (0, 0, 0))]
        + [pl.BlockSpec((rows, 2 * hidden), lambda n: (0, 0))] * 2
        + [pl.BlockSpec((tile, hidden), lambda n: (n, 0))],
        out_specs=[full, spread, spread],
        out_shape=[
            jax.ShapeDtypeStruct((rows, hidden), BF16),
            jax.ShapeDtypeStruct((2, tok_rows, width), BF16),
            jax.ShapeDtypeStruct((2, tok_rows, width), BF16),
        ],
        compiler_params=pltpu.CompilerParams(vmem_limit_bytes=32 * 1024 * 1024),
        cost_estimate=NO_COST,
    )(slot_of, *parts, weight)


def up_grad_kernel(*refs):
    count = (len(refs) - 1) // 2
    total = None
    for left, right in zip(refs[:count], refs[count:-1]):
        term = dot_f32(left[...], right[...], CONTRACT_ROWS)
        total = term if total is None else total + term
    refs[-1][...] = total.astype(BF16)


def down_grad_kernel(*refs):
    count = (len(refs) - 2) // 3
    out_ref, hidden_ref = refs[-2:]

    @pl.when(pl.program_id(0) == 0)
    def _():
        for index, (first, second) in enumerate(zip(refs[count : 2 * count], refs[2 * count : -2])):
            preact = first[...].astype(F32) + second[...].astype(F32)
            hidden_ref[index] = (preact * jax.nn.sigmoid(preact)).astype(BF16)

    total = None
    for index, left in enumerate(refs[:count]):
        term = dot_f32(left[...], hidden_ref[index], CONTRACT_ROWS)
        total = term if total is None else total + term
    out_ref[...] = total.astype(BF16)


def weight_grad(kernel, hidden, lefts, rights, scratch_shapes):
    rows, width = lefts[0].shape
    count = len(lefts)
    tile = 256
    return pl.pallas_call(
        kernel,
        grid=(width // tile,),
        in_specs=[pl.BlockSpec((rows, tile), lambda n: (0, n))] * count
        + [pl.BlockSpec((rows, hidden), lambda n: (0, 0))] * len(rights),
        out_specs=pl.BlockSpec((tile, hidden), lambda n: (n, 0)),
        out_shape=jax.ShapeDtypeStruct((width, hidden), BF16),
        scratch_shapes=scratch_shapes,
        compiler_params=pltpu.CompilerParams(vmem_limit_bytes=32 * 1024 * 1024),
        cost_estimate=NO_COST,
    )(*lefts, *rights)


def slots_and_gates(routing, own, limit, top_count):
    ids = routing[:, :, :top_count]
    levels = routing[:, :, top_count:].astype(F32)
    tok_rows = ids.shape[1]
    named = ids == own
    match = jnp.any(named, axis=2)
    gates = jnp.sum(jnp.where(named, levels, 0.0), axis=2) / jnp.sum(levels, axis=2)
    before = jnp.arange(tok_rows)[:, None] < jnp.arange(tok_rows)[None, :]
    rank = dot_f32(match.astype(BF16), before.astype(BF16)).astype(jnp.int32)
    return jnp.where(match & (rank < limit), rank, -1), gates


def grouped(tokens, cotangent, expert_ids, gate_levels, capacity, up_weight, down_weight):
    top_count = expert_ids.shape[1]
    slots = tokens.shape[0] * top_count // capacity.shape[0]
    own = lax.axis_index("expert")
    z = own // (NX * NC)
    inner = (z > 0) & (z < NZ - 1)
    who = own.astype(jnp.int32).reshape(1)
    weight_up, weight_down = up_weight[0], down_weight[0]

    hidden_units = weight_up.shape[1]

    rows_in, rows_cot, slot_of, parts, act, chip = ([None] * NZ for _ in range(6))

    def forth(s, *blocks):
        rows_in[s], rows_cot[s], part, slot_of[s] = front(
            blocks, who, capacity, weight_up, weight_down, slots, top_count
        )
        parts[s] = (part, swap_dp(part))

    def back_again(s, *earlier):
        pair = tie(parts[s], *earlier)
        act[s], keep, send = back(slot_of[s], pair, weight_up, slots)
        chip[s] = add(keep, swap_core(send))

    block = joined(tokens, cotangent, expert_ids, gate_levels)
    x_own = swap_x(block)
    near = along_z(block, NEIGHBOUR)
    two_in = along_z(block, MIDDLE)
    own_core = swap_core(block)

    near, two_in = tie((near, two_in), x_own)
    x_near = swap_x(near)
    far_in = along_z(near, MIDDLE)
    two_out = along_z(two_in, OUTWARD)
    near_core = swap_core(near)
    forth(0, block, own_core, x_own, swap_core(x_own))

    two, two_in, far_in = tie(
        (jnp.where(inner, far_in, two_out), two_in, far_in), x_near, parts[0][0]
    )
    x_two = swap_x(two)
    far_out = along_z(far_in, OUTWARD)
    two_core = swap_core(two)
    forth(1, near, near_core, x_near, swap_core(x_near))

    far = tie(jnp.where(inner, two_in, far_out), x_two, parts[1][0], parts[0][1])
    x_far = swap_x(far)
    far_core = swap_core(far)
    forth(2, two, two_core, x_two, swap_core(x_two))
    back_again(0)

    own_send = tie(chip[0][1], x_far, parts[2][0], parts[1][1])
    back_own = swap_x(own_send)
    forth(3, far, far_core, x_far, swap_core(x_far))
    back_again(1)

    near_send = tie(chip[1][1], back_own, parts[3][0])
    back_near = swap_x(near_send)
    back_again(2)
    near_sum = add(chip[1][0], back_near)
    hop_near = swap_z(near_sum, 1)

    two_send = tie(chip[2][1], near_sum)
    back_two = swap_x(two_send)
    two_sum = add(chip[2][0], back_two)
    hop_two = swap_z(two_sum, 2)
    back_again(3, near_sum)
    down_grad = weight_grad(
        down_grad_kernel,
        hidden_units,
        tie(rows_cot, chip[3]),
        [p[0] for p in parts] + [p[1] for p in parts],
        [pltpu.VMEM((NZ, parts[0][0].shape[0], hidden_units), BF16)],
    )

    far_send = tie(chip[3][1], two_sum)
    back_far = swap_x(far_send)
    far_sum = add(chip[3][0], back_far)
    hop_far = swap_z(far_sum, 3)
    up_grad = weight_grad(up_grad_kernel, hidden_units, rows_in, act, [])
    own_sum = chip[0][0].astype(F32) + back_own.astype(F32)
    for hop in (hop_near, hop_two, hop_far):
        own_sum = own_sum + hop.astype(F32)
    token_grad = own_sum.astype(BF16)
    return token_grad, up_grad[None], down_grad[None]


def general(n_expert, tokens, cotangent, expert_ids, gate_levels, capacity, up_weight, down_weight):
    tok_rows, width = tokens.shape
    top_count = expert_ids.shape[1]
    slots = tok_rows * top_count // capacity.shape[0]
    row_count = n_expert * slots
    own = lax.axis_index("expert")
    weight_up, weight_down = up_weight[0], down_weight[0]

    routing = lax.all_gather(
        jnp.concatenate([expert_ids, gate_levels], axis=1), "expert", axis=0, tiled=False
    )
    tok_all = lax.all_gather(tokens, "expert", axis=0, tiled=False)
    cot_all = lax.all_gather(cotangent, "expert", axis=0, tiled=False)
    slot_of, gates = slots_and_gates(routing, own, capacity[own], top_count)
    placing = slot_of[:, None, :] == jnp.arange(slots, dtype=jnp.int32)[None, :, None]
    slot_gate = jnp.sum(jnp.where(placing, gates[:, None, :], 0.0), axis=2)
    placing = placing.astype(BF16)
    pick = (((2,), (1,)), ((0,), (0,)))
    rows_in = dot_f32(placing, tok_all, pick).astype(BF16).reshape(row_count, width)
    rows_cot = (slot_gate[:, :, None] * dot_f32(placing, cot_all, pick)).astype(BF16)
    rows_cot = rows_cot.reshape(row_count, width)
    preact = lax.psum(dot_f32(rows_in, weight_up).astype(BF16).astype(F32), "dp")
    hidden_cot = lax.psum(dot_f32(rows_cot, weight_down).astype(BF16).astype(F32), "dp")
    sigmoid = jax.nn.sigmoid(preact)
    hidden = (preact * sigmoid).astype(BF16)
    act = (hidden_cot * (sigmoid * (1.0 + preact * (1.0 - sigmoid)))).astype(BF16)
    row_grad = dot_f32(act, weight_up, CONTRACT_LAST).astype(BF16)
    spread = dot_f32(
        placing, row_grad.reshape(n_expert, slots, width), (((1,), (1,)), ((0,), (0,)))
    ).astype(BF16)
    token_grad = lax.psum_scatter(
        spread.reshape(n_expert * tok_rows, width), "expert", scatter_dimension=0, tiled=True
    )
    up_grad = dot_f32(rows_in, act, CONTRACT_ROWS).astype(BF16)[None]
    down_grad = dot_f32(rows_cot, hidden, CONTRACT_ROWS).astype(BF16)[None]
    return token_grad, up_grad, down_grad


def solution(mesh):
    n_dp, n_expert = mesh.shape["dp"], mesh.shape["expert"]
    if n_dp == 2 and n_expert == NZ * NX * NC:
        body = grouped
    else:
        body = functools.partial(general, n_expert)
    return jax.shard_map(
        body,
        mesh=mesh,
        in_specs=(
            P("expert", "dp"),
            P("expert", "dp"),
            P("expert", None),
            P("expert", None),
            P(),
            P("expert", "dp", None),
            P("expert", "dp", None),
        ),
        out_specs=(P("expert", "dp"), P("expert", "dp", None), P("expert", "dp", None)),
        check_vma=False,
    )
```

```python
import functools

import jax
import jax.numpy as jnp
from jax import lax
from jax.experimental import pallas as pl
from jax.experimental.pallas import tpu as pltpu
from jax.sharding import PartitionSpec as P

F32 = jnp.float32
BF16 = jnp.bfloat16
CONTRACT_ROWS = (((0,), (0,)), ((), ()))
CONTRACT_LAST = (((1,), (1,)), ((), ()))

NO_COST = pl.CostEstimate(flops=0, bytes_accessed=0, transcendentals=0)
SOME_COST = pl.CostEstimate(flops=0, bytes_accessed=1 << 23, transcendentals=0)

NZ, NX, NC = 4, 2, 2


def dot_f32(left, right, dims=(((1,), (0,)), ((), ()))):
    return lax.dot_general(left, right, dims, preferred_element_type=F32)


def along_z(value, pairs):
    perm = [
        ((a * NX + x) * NC + c, (b * NX + x) * NC + c)
        for a, b in pairs
        for x in range(NX)
        for c in range(NC)
    ]
    return lax.ppermute(value, "expert", perm)


def swap_z(value, distance):
    step = distance * NX * NC
    return lax.ppermute(value, "expert", [(i, i ^ step) for i in range(NZ * NX * NC)])


def swap_x(value):
    return lax.ppermute(value, "expert", [(i, i ^ NC) for i in range(NZ * NX * NC)])


def swap_core(value):
    return lax.ppermute(value, "expert", [(i, i ^ 1) for i in range(NZ * NX * NC)])


def swap_dp(value):
    return lax.ppermute(value, "dp", [(0, 1), (1, 0)])


NEIGHBOUR = ((0, 1), (1, 0), (2, 3), (3, 2))
MIDDLE = ((1, 2), (2, 1))
OUTWARD = ((1, 0), (2, 3))


def tie(value, *earlier):
    return lax.optimization_barrier((value, earlier))[0]


def add(left, right):
    return (left.astype(F32) + right.astype(F32)).astype(BF16)


def placing_of(slot_row, slots):
    return slot_row == lax.broadcasted_iota(jnp.int32, (slots, slot_row.shape[1]), 0)


LANES = 128


def joined(tokens, cotangent, expert_ids, gate_levels):
    gap = LANES // 2 - expert_ids.shape[1]
    table = jnp.pad(expert_ids, ((0, 0), (0, gap + LANES // 2)))
    table = table + jnp.pad(gate_levels, ((0, 0), (LANES // 2, gap)))
    return jnp.concatenate([tokens, cotangent, table.astype(BF16)], axis=1)


def read_routing(meta, own, limit, top_count):
    tok_rows = meta.shape[0]
    ids = meta.astype(F32)
    levels = pltpu.roll(ids, LANES // 2, 1)
    choice = lax.broadcasted_iota(jnp.int32, ids.shape, 1) < top_count
    named = choice & (ids == own)
    ones = jnp.ones((8, LANES), BF16)
    match = dot_f32(ones, jnp.where(named, 1.0, 0.0).astype(BF16), CONTRACT_LAST)
    level = dot_f32(ones, jnp.where(named, levels, 0.0).astype(BF16), CONTRACT_LAST)
    total = dot_f32(ones, jnp.where(choice, levels, 0.0).astype(BF16), CONTRACT_LAST)
    square = (tok_rows, tok_rows)
    before = lax.broadcasted_iota(jnp.int32, square, 0) < lax.broadcasted_iota(jnp.int32, square, 1)
    rank = dot_f32(match.astype(BF16), jnp.where(before, 1.0, 0.0).astype(BF16))
    kept = (match > 0.5) & (rank < limit)
    return jnp.where(kept, rank, -1.0).astype(jnp.int32), level / total


def front_kernel(top_count, slots, own_ref, capacity_ref, *refs):
    metas, tok_blocks, cot_blocks = refs[:4], refs[4:8], refs[8:12]
    up_ref, down_ref, rows_ref, rows_cot_ref, slot_ref = refs[12:17]
    part_refs, (gates, total) = refs[17:-2], refs[-2:]
    step, hidden = pl.program_id(0), up_ref.shape[1]

    @pl.when(step == 0)
    def _():
        own = own_ref[0].astype(F32)
        limit = capacity_ref[own_ref[0]].astype(F32)
        for index, meta in enumerate(metas):
            slot, gate = read_routing(meta[...], own, limit, top_count)
            slot_ref[index] = slot
            gates[index] = gate

    for index in range(4):
        hit = placing_of(slot_ref[index, 0:1, :], slots)
        placing = jnp.where(hit, 1.0, 0.0).astype(BF16)
        gate = jnp.sum(jnp.where(hit, gates[index, 0:1, :], 0.0), axis=1, keepdims=True)
        here = slice(index * slots, (index + 1) * slots)
        rows_ref[here, :] = dot_f32(placing, tok_blocks[index][...]).astype(BF16)
        rows_cot_ref[here, :] = (gate * dot_f32(placing, cot_blocks[index][...])).astype(BF16)
    products = (dot_f32(rows_ref[...], up_ref[...]), dot_f32(rows_cot_ref[...], down_ref[...]))

    @pl.when(step == 0)
    def _():
        for half, product in enumerate(products):
            total[half] = product

    @pl.when(step > 0)
    def _():
        for half, product in enumerate(products):
            total[half] += product

    @pl.when(step == pl.num_programs(0) - 1)
    def _():
        for half in range(2):
            for piece, part_ref in enumerate(part_refs):
                height = part_ref.shape[0]
                rows = slice(piece * height, (piece + 1) * height)
                part_ref[:, half * hidden : (half + 1) * hidden] = total[half, rows].astype(BF16)


def front(blocks, own, capacity, weight_up, weight_down, slots, top_count, pieces):
    tok_rows = blocks[0].shape[0]
    width, hidden = weight_up.shape
    rows = 4 * slots
    tile = width // 2
    weight = pl.BlockSpec((tile, hidden), lambda k: (k, 0))
    picked = pl.BlockSpec((rows, tile), lambda k: (0, k))
    return pl.pallas_call(
        functools.partial(front_kernel, top_count, slots),
        grid=(width // tile,),
        in_specs=[pl.BlockSpec(memory_space=pltpu.SMEM)] * 2
        + [pl.BlockSpec((tok_rows, LANES), lambda k: (0, 2 * width // LANES))] * 4
        + [pl.BlockSpec((tok_rows, tile), lambda k: (0, k))] * 4
        + [pl.BlockSpec((tok_rows, tile), lambda k: (0, width // tile + k))] * 4
        + [weight, weight],
        out_specs=[
            picked,
            picked,
            pl.BlockSpec((4, 8, tok_rows), lambda k: (0, 0, 0)),
        ]
        + [pl.BlockSpec((rows // pieces, 2 * hidden), lambda k: (0, 0))] * pieces,
        out_shape=[
            jax.ShapeDtypeStruct((rows, width), BF16),
            jax.ShapeDtypeStruct((rows, width), BF16),
            jax.ShapeDtypeStruct((4, 8, tok_rows), jnp.int32),
        ]
        + [jax.ShapeDtypeStruct((rows // pieces, 2 * hidden), BF16)] * pieces,
        scratch_shapes=[
            pltpu.VMEM((4, 8, tok_rows), F32),
            pltpu.VMEM((2, rows, hidden), F32),
        ],
        compiler_params=pltpu.CompilerParams(vmem_limit_bytes=32 * 1024 * 1024),
        cost_estimate=NO_COST,
    )(own, capacity, *blocks, *blocks, *blocks, weight_up, weight_down)


def back_kernel(slots, first, slot_ref, part_a, part_b, weight_ref, act_ref, keep_ref, send_ref):
    @pl.when(pl.program_id(0) == 0)
    def _():
        hidden = act_ref.shape[1]
        preact = part_a[:, :hidden].astype(F32) + part_b[:, :hidden].astype(F32)
        hidden_cot = part_a[:, hidden:].astype(F32) + part_b[:, hidden:].astype(F32)
        sigmoid = jax.nn.sigmoid(preact)
        act_ref[...] = (hidden_cot * (sigmoid * (1.0 + preact * (1.0 - sigmoid)))).astype(BF16)

    back = dot_f32(act_ref[...], weight_ref[...], CONTRACT_LAST).astype(BF16)
    for index in range(act_ref.shape[0] // slots):
        hit = placing_of(slot_ref[first + index, 0:1, :], slots)
        placing = jnp.where(hit, 1.0, 0.0).astype(BF16)
        spread = dot_f32(placing, back[index * slots : (index + 1) * slots], CONTRACT_ROWS)
        out_ref = send_ref if index % 2 else keep_ref
        out_ref[index // 2] = spread.astype(BF16)


def back(slot_of, parts, weight, slots, first=0, cost=None):
    tok_rows = slot_of.shape[2]
    width, hidden = weight.shape
    rows = parts[0].shape[0]
    pairs = rows // (2 * slots)
    tile = width // 2
    full = pl.BlockSpec((rows, hidden), lambda n: (0, 0))
    spread = pl.BlockSpec((pairs, tok_rows, tile), lambda n: (0, 0, n))
    return pl.pallas_call(
        functools.partial(back_kernel, slots, first),
        grid=(width // tile,),
        in_specs=[pl.BlockSpec((4, 8, tok_rows), lambda n: (0, 0, 0))]
        + [pl.BlockSpec((rows, 2 * hidden), lambda n: (0, 0))] * 2
        + [pl.BlockSpec((tile, hidden), lambda n: (n, 0))],
        out_specs=[full, spread, spread],
        out_shape=[
            jax.ShapeDtypeStruct((rows, hidden), BF16),
            jax.ShapeDtypeStruct((pairs, tok_rows, width), BF16),
            jax.ShapeDtypeStruct((pairs, tok_rows, width), BF16),
        ],
        compiler_params=pltpu.CompilerParams(vmem_limit_bytes=32 * 1024 * 1024),
        cost_estimate=cost or NO_COST,
    )(slot_of, *parts, weight)


def up_grad_kernel(*refs):
    count = (len(refs) - 1) // 2
    total = None
    for left, right in zip(refs[:count], refs[count:-1]):
        term = dot_f32(left[...], right[...], CONTRACT_ROWS)
        total = term if total is None else total + term
    refs[-1][...] = total.astype(BF16)


def down_grad_kernel(*refs):
    count = (len(refs) - 2) // 3
    out_ref, hidden_ref = refs[-2:]
    heights = [left.shape[0] for left in refs[:count]]
    spans = [slice(sum(heights[:i]), sum(heights[: i + 1])) for i in range(count)]

    @pl.when(pl.program_id(0) == 0)
    def _():
        for span, first, second in zip(spans, refs[count : 2 * count], refs[2 * count : -2]):
            preact = first[...].astype(F32) + second[...].astype(F32)
            hidden_ref[span, :] = (preact * jax.nn.sigmoid(preact)).astype(BF16)

    total = None
    for span, left in zip(spans, refs[:count]):
        term = dot_f32(left[...], hidden_ref[span, :], CONTRACT_ROWS)
        total = term if total is None else total + term
    out_ref[...] = total.astype(BF16)


def weight_grad(kernel, hidden, lefts, pieces, rights, scratch_shapes):
    width = lefts[0].shape[1]
    tile = 256
    in_specs, operands = [], []
    for index, left in enumerate(lefts):
        count = pieces if index == len(lefts) - 1 else 1
        for piece in range(count):
            in_specs.append(pl.BlockSpec((left.shape[0] // count, tile), lambda n, piece=piece: (piece, n)))
            operands.append(left)
    for right in rights:
        in_specs.append(pl.BlockSpec((right.shape[0], hidden), lambda n: (0, 0)))
        operands.append(right)
    return pl.pallas_call(
        kernel,
        grid=(width // tile,),
        in_specs=in_specs,
        out_specs=pl.BlockSpec((tile, hidden), lambda n: (n, 0)),
        out_shape=jax.ShapeDtypeStruct((width, hidden), BF16),
        scratch_shapes=scratch_shapes,
        compiler_params=pltpu.CompilerParams(vmem_limit_bytes=32 * 1024 * 1024),
        cost_estimate=NO_COST,
    )(*operands)


def slots_and_gates(routing, own, limit, top_count):
    ids = routing[:, :, :top_count]
    levels = routing[:, :, top_count:].astype(F32)
    tok_rows = ids.shape[1]
    named = ids == own
    match = jnp.any(named, axis=2)
    gates = jnp.sum(jnp.where(named, levels, 0.0), axis=2) / jnp.sum(levels, axis=2)
    before = jnp.arange(tok_rows)[:, None] < jnp.arange(tok_rows)[None, :]
    rank = dot_f32(match.astype(BF16), before.astype(BF16)).astype(jnp.int32)
    return jnp.where(match & (rank < limit), rank, -1), gates


def grouped(tokens, cotangent, expert_ids, gate_levels, capacity, up_weight, down_weight):
    top_count = expert_ids.shape[1]
    slots = tokens.shape[0] * top_count // capacity.shape[0]
    own = lax.axis_index("expert")
    z = own // (NX * NC)
    inner = (z > 0) & (z < NZ - 1)
    who = own.astype(jnp.int32).reshape(1)
    weight_up, weight_down = up_weight[0], down_weight[0]

    hidden_units = weight_up.shape[1]

    rows_in, rows_cot, slot_of, parts, act, chip = ([None] * NZ for _ in range(6))

    def forth(s, *blocks):
        pieces = 2 if s == NZ - 1 else 1
        rows_in[s], rows_cot[s], slot_of[s], *part = front(
            blocks, who, capacity, weight_up, weight_down, slots, top_count, pieces
        )
        swapped = [swap_dp(part[-1])]
        if pieces == 2:
            swapped.append(swap_dp(tie(part[0], swapped[0])))
        parts[s] = (*part, *swapped)

    def back_again(s, *earlier):
        pair = tie(parts[s], *earlier)
        act[s], keep, send = back(slot_of[s], pair, weight_up, slots)
        chip[s] = add(keep, swap_core(send))

    block = joined(tokens, cotangent, expert_ids, gate_levels)
    x_own = swap_x(block)
    near = along_z(block, NEIGHBOUR)
    two_in = along_z(block, MIDDLE)
    own_core = swap_core(block)

    near, two_in = tie((near, two_in), x_own)
    x_near = swap_x(near)
    far_in = along_z(near, MIDDLE)
    two_out = along_z(two_in, OUTWARD)
    near_core = swap_core(near)
    forth(0, block, own_core, x_own, swap_core(x_own))

    two, two_in, far_in = tie(
        (jnp.where(inner, far_in, two_out), two_in, far_in), x_near, parts[0][0]
    )
    x_two = swap_x(two)
    far_out = along_z(far_in, OUTWARD)
    two_core = swap_core(two)
    forth(1, near, near_core, x_near, swap_core(x_near))

    far = tie(jnp.where(inner, two_in, far_out), x_two, parts[1][0], parts[0][1])
    x_far = swap_x(far)
    far_core = swap_core(far)
    forth(2, two, two_core, x_two, swap_core(x_two))
    back_again(0)

    own_send = tie(chip[0][1], x_far, parts[2][0], parts[1][1])
    back_own = swap_x(own_send)
    forth(3, far, far_core, x_far, swap_core(x_far))
    back_again(1)

    near_send = tie(chip[1][1], back_own, parts[3][0])
    back_near = swap_x(near_send)
    back_again(2)
    near_sum = add(chip[1][0], back_near)
    hop_near = swap_z(near_sum, 1)

    two_send = tie(chip[2][1], near_sum)
    back_two = swap_x(two_send)
    two_sum = add(chip[2][0], back_two)
    hop_two = swap_z(two_sum, 2)
    part_own, part_other, dp_other, dp_own = parts[3]
    act_other, keep, send = back(
        slot_of[3], tie((part_other, dp_other), near_sum, chip[2]), weight_up, slots, 2
    )
    other_sum = add(keep[0], swap_core(send)[0])
    far_send = tie(other_sum, two_sum)
    back_far = swap_x(far_send)
    act_own, keep, send = back(slot_of[3], tie((part_own, dp_own), other_sum), weight_up, slots)
    far_sum = add(add(keep[0], swap_core(send)[0]), back_far)
    hop_far = swap_z(far_sum, 3)
    whole = parts[:3]
    down_grad = weight_grad(
        down_grad_kernel,
        hidden_units,
        tie(rows_cot, far_sum),
        2,
        [p[0] for p in whole] + [part_own, part_other] + [p[1] for p in whole] + [dp_own, dp_other],
        [pltpu.VMEM((NZ * parts[0][0].shape[0], hidden_units), BF16)],
    )
    up_grad = weight_grad(up_grad_kernel, hidden_units, rows_in, 2, act[:3] + [act_own, act_other], [])
    own_sum = chip[0][0].astype(F32) + back_own.astype(F32)
    for hop in (hop_near, hop_two, hop_far):
        own_sum = own_sum + hop.astype(F32)
    token_grad = own_sum.astype(BF16)
    return token_grad, up_grad[None], down_grad[None]


def general(n_expert, tokens, cotangent, expert_ids, gate_levels, capacity, up_weight, down_weight):
    tok_rows, width = tokens.shape
    top_count = expert_ids.shape[1]
    slots = tok_rows * top_count // capacity.shape[0]
    row_count = n_expert * slots
    own = lax.axis_index("expert")
    weight_up, weight_down = up_weight[0], down_weight[0]

    routing = lax.all_gather(
        jnp.concatenate([expert_ids, gate_levels], axis=1), "expert", axis=0, tiled=False
    )
    tok_all = lax.all_gather(tokens, "expert", axis=0, tiled=False)
    cot_all = lax.all_gather(cotangent, "expert", axis=0, tiled=False)
    slot_of, gates = slots_and_gates(routing, own, capacity[own], top_count)
    placing = slot_of[:, None, :] == jnp.arange(slots, dtype=jnp.int32)[None, :, None]
    slot_gate = jnp.sum(jnp.where(placing, gates[:, None, :], 0.0), axis=2)
    placing = placing.astype(BF16)
    pick = (((2,), (1,)), ((0,), (0,)))
    rows_in = dot_f32(placing, tok_all, pick).astype(BF16).reshape(row_count, width)
    rows_cot = (slot_gate[:, :, None] * dot_f32(placing, cot_all, pick)).astype(BF16)
    rows_cot = rows_cot.reshape(row_count, width)
    preact = lax.psum(dot_f32(rows_in, weight_up).astype(BF16).astype(F32), "dp")
    hidden_cot = lax.psum(dot_f32(rows_cot, weight_down).astype(BF16).astype(F32), "dp")
    sigmoid = jax.nn.sigmoid(preact)
    hidden = (preact * sigmoid).astype(BF16)
    act = (hidden_cot * (sigmoid * (1.0 + preact * (1.0 - sigmoid)))).astype(BF16)
    row_grad = dot_f32(act, weight_up, CONTRACT_LAST).astype(BF16)
    spread = dot_f32(
        placing, row_grad.reshape(n_expert, slots, width), (((1,), (1,)), ((0,), (0,)))
    ).astype(BF16)
    token_grad = lax.psum_scatter(
        spread.reshape(n_expert * tok_rows, width), "expert", scatter_dimension=0, tiled=True
    )
    up_grad = dot_f32(rows_in, act, CONTRACT_ROWS).astype(BF16)[None]
    down_grad = dot_f32(rows_cot, hidden, CONTRACT_ROWS).astype(BF16)[None]
    return token_grad, up_grad, down_grad


def solution(mesh):
    n_dp, n_expert = mesh.shape["dp"], mesh.shape["expert"]
    if n_dp == 2 and n_expert == NZ * NX * NC:
        body = grouped
    else:
        body = functools.partial(general, n_expert)
    return jax.shard_map(
        body,
        mesh=mesh,
        in_specs=(
            P("expert", "dp"),
            P("expert", "dp"),
            P("expert", None),
            P("expert", None),
            P(),
            P("expert", "dp", None),
            P("expert", "dp", None),
        ),
        out_specs=(P("expert", "dp"), P("expert", "dp", None), P("expert", "dp", None)),
        check_vma=False,
    )
```

```python
import functools

import jax
import jax.numpy as jnp
from jax import lax
from jax.experimental import pallas as pl
from jax.experimental.pallas import tpu as pltpu
from jax.sharding import PartitionSpec as P

F32 = jnp.float32
BF16 = jnp.bfloat16
CONTRACT_ROWS = (((0,), (0,)), ((), ()))
CONTRACT_LAST = (((1,), (1,)), ((), ()))

NO_COST = pl.CostEstimate(flops=0, bytes_accessed=0, transcendentals=0)
SOME_COST = pl.CostEstimate(flops=0, bytes_accessed=1 << 23, transcendentals=0)

NZ, NX, NC = 4, 2, 2


def dot_f32(left, right, dims=(((1,), (0,)), ((), ()))):
    return lax.dot_general(left, right, dims, preferred_element_type=F32)


def along_z(value, pairs):
    perm = [
        ((a * NX + x) * NC + c, (b * NX + x) * NC + c)
        for a, b in pairs
        for x in range(NX)
        for c in range(NC)
    ]
    return lax.ppermute(value, "expert", perm)


def swap_z(value, distance):
    step = distance * NX * NC
    return lax.ppermute(value, "expert", [(i, i ^ step) for i in range(NZ * NX * NC)])


def swap_x(value):
    return lax.ppermute(value, "expert", [(i, i ^ NC) for i in range(NZ * NX * NC)])


def swap_core(value):
    return lax.ppermute(value, "expert", [(i, i ^ 1) for i in range(NZ * NX * NC)])


def swap_dp(value):
    return lax.ppermute(value, "dp", [(0, 1), (1, 0)])


NEIGHBOUR = ((0, 1), (1, 0), (2, 3), (3, 2))
MIDDLE = ((1, 2), (2, 1))
OUTWARD = ((1, 0), (2, 3))


def tie(value, *earlier):
    return lax.optimization_barrier((value, earlier))[0]


def add(left, right):
    return (left.astype(F32) + right.astype(F32)).astype(BF16)


def placing_of(slot_row, slots):
    return slot_row == lax.broadcasted_iota(jnp.int32, (slots, slot_row.shape[1]), 0)


LANES = 128


def joined(tokens, cotangent, expert_ids, gate_levels):
    gap = LANES // 2 - expert_ids.shape[1]
    table = jnp.pad(expert_ids, ((0, 0), (0, gap + LANES // 2)))
    table = table + jnp.pad(gate_levels, ((0, 0), (LANES // 2, gap)))
    return jnp.concatenate([tokens, cotangent, table.astype(BF16)], axis=1)


def read_routing(meta, own, limit, top_count):
    tok_rows = meta.shape[0]
    ids = meta.astype(F32)
    levels = pltpu.roll(ids, LANES // 2, 1)
    choice = lax.broadcasted_iota(jnp.int32, ids.shape, 1) < top_count
    named = choice & (ids == own)
    ones = jnp.ones((8, LANES), BF16)
    match = dot_f32(ones, jnp.where(named, 1.0, 0.0).astype(BF16), CONTRACT_LAST)
    level = dot_f32(ones, jnp.where(named, levels, 0.0).astype(BF16), CONTRACT_LAST)
    total = dot_f32(ones, jnp.where(choice, levels, 0.0).astype(BF16), CONTRACT_LAST)
    square = (tok_rows, tok_rows)
    before = lax.broadcasted_iota(jnp.int32, square, 0) < lax.broadcasted_iota(jnp.int32, square, 1)
    rank = dot_f32(match.astype(BF16), jnp.where(before, 1.0, 0.0).astype(BF16))
    kept = (match > 0.5) & (rank < limit)
    return jnp.where(kept, rank, -1.0).astype(jnp.int32), level / total


def front_kernel(top_count, slots, own_ref, capacity_ref, *refs):
    metas, tok_blocks, cot_blocks = refs[:4], refs[4:8], refs[8:12]
    up_ref, down_ref, rows_ref, rows_cot_ref, slot_ref = refs[12:17]
    part_refs, (gates, total) = refs[17:-2], refs[-2:]
    step, hidden = pl.program_id(0), up_ref.shape[1]

    @pl.when(step == 0)
    def _():
        own = own_ref[0].astype(F32)
        limit = capacity_ref[own_ref[0]].astype(F32)
        for index, meta in enumerate(metas):
            slot, gate = read_routing(meta[...], own, limit, top_count)
            slot_ref[index] = slot
            gates[index] = gate

    for index in range(4):
        hit = placing_of(slot_ref[index, 0:1, :], slots)
        placing = jnp.where(hit, 1.0, 0.0).astype(BF16)
        gate = jnp.sum(jnp.where(hit, gates[index, 0:1, :], 0.0), axis=1, keepdims=True)
        here = slice(index * slots, (index + 1) * slots)
        rows_ref[here, :] = dot_f32(placing, tok_blocks[index][...]).astype(BF16)
        rows_cot_ref[here, :] = (gate * dot_f32(placing, cot_blocks[index][...])).astype(BF16)
    products = (dot_f32(rows_ref[...], up_ref[...]), dot_f32(rows_cot_ref[...], down_ref[...]))

    @pl.when(step == 0)
    def _():
        for half, product in enumerate(products):
            total[half] = product

    @pl.when(step > 0)
    def _():
        for half, product in enumerate(products):
            total[half] += product

    @pl.when(step == pl.num_programs(0) - 1)
    def _():
        for half in range(2):
            for piece, part_ref in enumerate(part_refs):
                height = part_ref.shape[0]
                rows = slice(piece * height, (piece + 1) * height)
                part_ref[:, half * hidden : (half + 1) * hidden] = total[half, rows].astype(BF16)


def front(blocks, own, capacity, weight_up, weight_down, slots, top_count, pieces):
    tok_rows = blocks[0].shape[0]
    width, hidden = weight_up.shape
    rows = 4 * slots
    tile = width // 2
    weight = pl.BlockSpec((tile, hidden), lambda k: (k, 0))
    picked = pl.BlockSpec((rows, tile), lambda k: (0, k))
    return pl.pallas_call(
        functools.partial(front_kernel, top_count, slots),
        grid=(width // tile,),
        in_specs=[pl.BlockSpec(memory_space=pltpu.SMEM)] * 2
        + [pl.BlockSpec((tok_rows, LANES), lambda k: (0, 2 * width // LANES))] * 4
        + [pl.BlockSpec((tok_rows, tile), lambda k: (0, k))] * 4
        + [pl.BlockSpec((tok_rows, tile), lambda k: (0, width // tile + k))] * 4
        + [weight, weight],
        out_specs=[
            picked,
            picked,
            pl.BlockSpec((4, 8, tok_rows), lambda k: (0, 0, 0)),
        ]
        + [pl.BlockSpec((rows // pieces, 2 * hidden), lambda k: (0, 0))] * pieces,
        out_shape=[
            jax.ShapeDtypeStruct((rows, width), BF16),
            jax.ShapeDtypeStruct((rows, width), BF16),
            jax.ShapeDtypeStruct((4, 8, tok_rows), jnp.int32),
        ]
        + [jax.ShapeDtypeStruct((rows // pieces, 2 * hidden), BF16)] * pieces,
        scratch_shapes=[
            pltpu.VMEM((4, 8, tok_rows), F32),
            pltpu.VMEM((2, rows, hidden), F32),
        ],
        compiler_params=pltpu.CompilerParams(vmem_limit_bytes=32 * 1024 * 1024),
        cost_estimate=NO_COST,
    )(own, capacity, *blocks, *blocks, *blocks, weight_up, weight_down)


def back_kernel(slots, first, slot_ref, part_a, part_b, weight_ref, act_ref, keep_ref, send_ref):
    @pl.when(pl.program_id(0) == 0)
    def _():
        hidden = act_ref.shape[1]
        preact = part_a[:, :hidden].astype(F32) + part_b[:, :hidden].astype(F32)
        hidden_cot = part_a[:, hidden:].astype(F32) + part_b[:, hidden:].astype(F32)
        sigmoid = jax.nn.sigmoid(preact)
        act_ref[...] = (hidden_cot * (sigmoid * (1.0 + preact * (1.0 - sigmoid)))).astype(BF16)

    back = dot_f32(act_ref[...], weight_ref[...], CONTRACT_LAST).astype(BF16)
    for index in range(act_ref.shape[0] // slots):
        hit = placing_of(slot_ref[first + index, 0:1, :], slots)
        placing = jnp.where(hit, 1.0, 0.0).astype(BF16)
        spread = dot_f32(placing, back[index * slots : (index + 1) * slots], CONTRACT_ROWS)
        out_ref = send_ref if index % 2 else keep_ref
        out_ref[index // 2] = spread.astype(BF16)


def back(slot_of, parts, weight, slots, first=0, cost=None):
    tok_rows = slot_of.shape[2]
    width, hidden = weight.shape
    rows = parts[0].shape[0]
    pairs = rows // (2 * slots)
    tile = width // 2
    full = pl.BlockSpec((rows, hidden), lambda n: (0, 0))
    spread = pl.BlockSpec((pairs, tok_rows, tile), lambda n: (0, 0, n))
    return pl.pallas_call(
        functools.partial(back_kernel, slots, first),
        grid=(width // tile,),
        in_specs=[pl.BlockSpec((4, 8, tok_rows), lambda n: (0, 0, 0))]
        + [pl.BlockSpec((rows, 2 * hidden), lambda n: (0, 0))] * 2
        + [pl.BlockSpec((tile, hidden), lambda n: (n, 0))],
        out_specs=[full, spread, spread],
        out_shape=[
            jax.ShapeDtypeStruct((rows, hidden), BF16),
            jax.ShapeDtypeStruct((pairs, tok_rows, width), BF16),
            jax.ShapeDtypeStruct((pairs, tok_rows, width), BF16),
        ],
        compiler_params=pltpu.CompilerParams(vmem_limit_bytes=32 * 1024 * 1024),
        cost_estimate=cost or NO_COST,
    )(slot_of, *parts, weight)


def up_grad_kernel(*refs):
    count = (len(refs) - 1) // 2
    total = None
    for left, right in zip(refs[:count], refs[count:-1]):
        term = dot_f32(left[...], right[...], CONTRACT_ROWS)
        total = term if total is None else total + term
    refs[-1][...] = total.astype(BF16)


def down_grad_kernel(*refs):
    count = (len(refs) - 2) // 3
    out_ref, hidden_ref = refs[-2:]
    heights = [left.shape[0] for left in refs[:count]]
    spans = [slice(sum(heights[:i]), sum(heights[: i + 1])) for i in range(count)]

    @pl.when(pl.program_id(0) == 0)
    def _():
        for span, first, second in zip(spans, refs[count : 2 * count], refs[2 * count : -2]):
            preact = first[...].astype(F32) + second[...].astype(F32)
            hidden_ref[span, :] = (preact * jax.nn.sigmoid(preact)).astype(BF16)

    total = None
    for span, left in zip(spans, refs[:count]):
        term = dot_f32(left[...], hidden_ref[span, :], CONTRACT_ROWS)
        total = term if total is None else total + term
    out_ref[...] = total.astype(BF16)


def weight_grad(kernel, hidden, lefts, pieces, rights, scratch_shapes):
    width = lefts[0].shape[1]
    tile = 256
    in_specs, operands = [], []
    for index, left in enumerate(lefts):
        count = pieces if index == len(lefts) - 1 else 1
        for piece in range(count):
            in_specs.append(pl.BlockSpec((left.shape[0] // count, tile), lambda n, piece=piece: (piece, n)))
            operands.append(left)
    for right in rights:
        in_specs.append(pl.BlockSpec((right.shape[0], hidden), lambda n: (0, 0)))
        operands.append(right)
    return pl.pallas_call(
        kernel,
        grid=(width // tile,),
        in_specs=in_specs,
        out_specs=pl.BlockSpec((tile, hidden), lambda n: (n, 0)),
        out_shape=jax.ShapeDtypeStruct((width, hidden), BF16),
        scratch_shapes=scratch_shapes,
        compiler_params=pltpu.CompilerParams(vmem_limit_bytes=32 * 1024 * 1024),
        cost_estimate=NO_COST,
    )(*operands)


def slots_and_gates(routing, own, limit, top_count):
    ids = routing[:, :, :top_count]
    levels = routing[:, :, top_count:].astype(F32)
    tok_rows = ids.shape[1]
    named = ids == own
    match = jnp.any(named, axis=2)
    gates = jnp.sum(jnp.where(named, levels, 0.0), axis=2) / jnp.sum(levels, axis=2)
    before = jnp.arange(tok_rows)[:, None] < jnp.arange(tok_rows)[None, :]
    rank = dot_f32(match.astype(BF16), before.astype(BF16)).astype(jnp.int32)
    return jnp.where(match & (rank < limit), rank, -1), gates


def grouped(tokens, cotangent, expert_ids, gate_levels, capacity, up_weight, down_weight):
    top_count = expert_ids.shape[1]
    slots = tokens.shape[0] * top_count // capacity.shape[0]
    own = lax.axis_index("expert")
    z = own // (NX * NC)
    inner = (z > 0) & (z < NZ - 1)
    who = own.astype(jnp.int32).reshape(1)
    weight_up, weight_down = up_weight[0], down_weight[0]

    hidden_units = weight_up.shape[1]

    rows_in, rows_cot, slot_of, parts, act, chip = ([None] * NZ for _ in range(6))

    def forth(s, *blocks):
        pieces = 2 if s == NZ - 1 else 1
        rows_in[s], rows_cot[s], slot_of[s], *part = front(
            blocks, who, capacity, weight_up, weight_down, slots, top_count, pieces
        )
        swapped = [swap_dp(part[-1])]
        if pieces == 2:
            swapped.append(swap_dp(tie(part[0], swapped[0])))
        parts[s] = (*part, *swapped)

    def back_again(s, *earlier):
        pair = tie(parts[s], *earlier)
        act[s], keep, send = back(slot_of[s], pair, weight_up, slots)
        chip[s] = add(keep, swap_core(send))

    block = joined(tokens, cotangent, expert_ids, gate_levels)
    x_own = swap_x(block)
    near = along_z(block, NEIGHBOUR)
    two_in = along_z(block, MIDDLE)
    own_core = swap_core(block)

    near, two_in = tie((near, two_in), x_own)
    x_near = swap_x(near)
    far_in = along_z(near, MIDDLE)
    two_out = along_z(two_in, OUTWARD)
    near_core = swap_core(near)
    forth(0, block, own_core, x_own, swap_core(x_own))

    two, two_in, far_in = tie(
        (jnp.where(inner, far_in, two_out), two_in, far_in), x_near, parts[0][0]
    )
    x_two = swap_x(two)
    far_out = along_z(far_in, OUTWARD)
    two_core = swap_core(two)
    forth(1, near, near_core, x_near, swap_core(x_near))

    far = tie(jnp.where(inner, two_in, far_out), x_two, parts[1][0], parts[0][1])
    x_far = swap_x(far)
    far_core = swap_core(far)
    forth(2, two, two_core, x_two, swap_core(x_two))
    back_again(0)

    own_send = tie(chip[0][1], x_far, parts[2][0], parts[1][1])
    back_own = swap_x(own_send)
    forth(3, far, far_core, x_far, swap_core(x_far))
    back_again(1)

    near_send = tie(chip[1][1], back_own, parts[3][0])
    back_near = swap_x(near_send)
    back_again(2)
    near_sum = add(chip[1][0], back_near)
    hop_near = swap_z(near_sum, 1)

    two_send = tie(chip[2][1], near_sum)
    back_two = swap_x(two_send)
    two_sum = add(chip[2][0], back_two)
    hop_two = swap_z(two_sum, 2)
    part_own, part_other, dp_other, dp_own = parts[3]
    act_other, keep, send = back(
        slot_of[3], tie((part_other, dp_other), near_sum, chip[2]), weight_up, slots, 2
    )
    other_sum = add(keep[0], swap_core(send)[0])
    far_send = tie(other_sum, two_sum)
    back_far = swap_x(far_send)
    act_own, keep, send = back(slot_of[3], tie((part_own, dp_own), other_sum), weight_up, slots)
    far_sum = add(add(keep[0], swap_core(tie(send, hop_two))[0]), back_far)
    hop_far = swap_z(far_sum, 3)
    whole = parts[:3]
    down_grad = weight_grad(
        down_grad_kernel,
        hidden_units,
        tie(rows_cot, far_sum),
        2,
        [p[0] for p in whole] + [part_own, part_other] + [p[1] for p in whole] + [dp_own, dp_other],
        [pltpu.VMEM((NZ * parts[0][0].shape[0], hidden_units), BF16)],
    )
    up_grad = weight_grad(up_grad_kernel, hidden_units, rows_in, 2, act[:3] + [act_own, act_other], [])
    own_sum = chip[0][0].astype(F32) + back_own.astype(F32)
    for hop in (hop_near, hop_two, hop_far):
        own_sum = own_sum + hop.astype(F32)
    token_grad = own_sum.astype(BF16)
    return token_grad, up_grad[None], down_grad[None]


def general(n_expert, tokens, cotangent, expert_ids, gate_levels, capacity, up_weight, down_weight):
    tok_rows, width = tokens.shape
    top_count = expert_ids.shape[1]
    slots = tok_rows * top_count // capacity.shape[0]
    row_count = n_expert * slots
    own = lax.axis_index("expert")
    weight_up, weight_down = up_weight[0], down_weight[0]

    routing = lax.all_gather(
        jnp.concatenate([expert_ids, gate_levels], axis=1), "expert", axis=0, tiled=False
    )
    tok_all = lax.all_gather(tokens, "expert", axis=0, tiled=False)
    cot_all = lax.all_gather(cotangent, "expert", axis=0, tiled=False)
    slot_of, gates = slots_and_gates(routing, own, capacity[own], top_count)
    placing = slot_of[:, None, :] == jnp.arange(slots, dtype=jnp.int32)[None, :, None]
    slot_gate = jnp.sum(jnp.where(placing, gates[:, None, :], 0.0), axis=2)
    placing = placing.astype(BF16)
    pick = (((2,), (1,)), ((0,), (0,)))
    rows_in = dot_f32(placing, tok_all, pick).astype(BF16).reshape(row_count, width)
    rows_cot = (slot_gate[:, :, None] * dot_f32(placing, cot_all, pick)).astype(BF16)
    rows_cot = rows_cot.reshape(row_count, width)
    preact = lax.psum(dot_f32(rows_in, weight_up).astype(BF16).astype(F32), "dp")
    hidden_cot = lax.psum(dot_f32(rows_cot, weight_down).astype(BF16).astype(F32), "dp")
    sigmoid = jax.nn.sigmoid(preact)
    hidden = (preact * sigmoid).astype(BF16)
    act = (hidden_cot * (sigmoid * (1.0 + preact * (1.0 - sigmoid)))).astype(BF16)
    row_grad = dot_f32(act, weight_up, CONTRACT_LAST).astype(BF16)
    spread = dot_f32(
        placing, row_grad.reshape(n_expert, slots, width), (((1,), (1,)), ((0,), (0,)))
    ).astype(BF16)
    token_grad = lax.psum_scatter(
        spread.reshape(n_expert * tok_rows, width), "expert", scatter_dimension=0, tiled=True
    )
    up_grad = dot_f32(rows_in, act, CONTRACT_ROWS).astype(BF16)[None]
    down_grad = dot_f32(rows_cot, hidden, CONTRACT_ROWS).astype(BF16)[None]
    return token_grad, up_grad, down_grad


def solution(mesh):
    n_dp, n_expert = mesh.shape["dp"], mesh.shape["expert"]
    if n_dp == 2 and n_expert == NZ * NX * NC:
        body = grouped
    else:
        body = functools.partial(general, n_expert)
    return jax.shard_map(
        body,
        mesh=mesh,
        in_specs=(
            P("expert", "dp"),
            P("expert", "dp"),
            P("expert", None),
            P("expert", None),
            P(),
            P("expert", "dp", None),
            P("expert", "dp", None),
        ),
        out_specs=(P("expert", "dp"), P("expert", "dp", None), P("expert", "dp", None)),
        check_vma=False,
    )
```

```python
import functools

import jax
import jax.numpy as jnp
from jax import lax
from jax.experimental import pallas as pl
from jax.experimental.pallas import tpu as pltpu
from jax.sharding import PartitionSpec as P

F32 = jnp.float32
BF16 = jnp.bfloat16
CONTRACT_ROWS = (((0,), (0,)), ((), ()))
CONTRACT_LAST = (((1,), (1,)), ((), ()))

NO_COST = pl.CostEstimate(flops=0, bytes_accessed=0, transcendentals=0)
SOME_COST = pl.CostEstimate(flops=0, bytes_accessed=1 << 23, transcendentals=0)

NZ, NX, NC = 4, 2, 2


def dot_f32(left, right, dims=(((1,), (0,)), ((), ()))):
    return lax.dot_general(left, right, dims, preferred_element_type=F32)


def along_z(value, pairs):
    perm = [
        ((a * NX + x) * NC + c, (b * NX + x) * NC + c)
        for a, b in pairs
        for x in range(NX)
        for c in range(NC)
    ]
    return lax.ppermute(value, "expert", perm)


def swap_z(value, distance):
    step = distance * NX * NC
    return lax.ppermute(value, "expert", [(i, i ^ step) for i in range(NZ * NX * NC)])


def swap_x(value):
    return lax.ppermute(value, "expert", [(i, i ^ NC) for i in range(NZ * NX * NC)])


def swap_core(value):
    return lax.ppermute(value, "expert", [(i, i ^ 1) for i in range(NZ * NX * NC)])


def swap_dp(value):
    return lax.ppermute(value, "dp", [(0, 1), (1, 0)])


NEIGHBOUR = ((0, 1), (1, 0), (2, 3), (3, 2))
MIDDLE = ((1, 2), (2, 1))
OUTWARD = ((1, 0), (2, 3))


def tie(value, *earlier):
    return lax.optimization_barrier((value, earlier))[0]


def add(left, right):
    return (left.astype(F32) + right.astype(F32)).astype(BF16)


def placing_of(slot_row, slots):
    return slot_row == lax.broadcasted_iota(jnp.int32, (slots, slot_row.shape[1]), 0)


LANES = 128


def joined(tokens, cotangent, expert_ids, gate_levels):
    gap = LANES // 2 - expert_ids.shape[1]
    table = jnp.pad(expert_ids, ((0, 0), (0, gap + LANES // 2)))
    table = table + jnp.pad(gate_levels, ((0, 0), (LANES // 2, gap)))
    return jnp.concatenate([tokens, cotangent, table.astype(BF16)], axis=1)


def read_routing(meta, own, limit, top_count):
    tok_rows = meta.shape[0]
    ids = meta.astype(F32)
    levels = pltpu.roll(ids, LANES // 2, 1)
    choice = lax.broadcasted_iota(jnp.int32, ids.shape, 1) < top_count
    named = choice & (ids == own)
    ones = jnp.ones((8, LANES), BF16)
    match = dot_f32(ones, jnp.where(named, 1.0, 0.0).astype(BF16), CONTRACT_LAST)
    level = dot_f32(ones, jnp.where(named, levels, 0.0).astype(BF16), CONTRACT_LAST)
    total = dot_f32(ones, jnp.where(choice, levels, 0.0).astype(BF16), CONTRACT_LAST)
    square = (tok_rows, tok_rows)
    before = lax.broadcasted_iota(jnp.int32, square, 0) < lax.broadcasted_iota(jnp.int32, square, 1)
    rank = dot_f32(match.astype(BF16), jnp.where(before, 1.0, 0.0).astype(BF16))
    kept = (match > 0.5) & (rank < limit)
    return jnp.where(kept, rank, -1.0).astype(jnp.int32), level / total


def front_kernel(top_count, slots, own_ref, capacity_ref, *refs):
    metas, tok_blocks, cot_blocks = refs[:4], refs[4:8], refs[8:12]
    up_ref, down_ref, rows_ref, rows_cot_ref, slot_ref = refs[12:17]
    part_refs, (gates, total) = refs[17:-2], refs[-2:]
    step, hidden = pl.program_id(0), up_ref.shape[1]

    @pl.when(step == 0)
    def _():
        own = own_ref[0].astype(F32)
        limit = capacity_ref[own_ref[0]].astype(F32)
        for index, meta in enumerate(metas):
            slot, gate = read_routing(meta[...], own, limit, top_count)
            slot_ref[index] = slot
            gates[index] = gate

    for index in range(4):
        hit = placing_of(slot_ref[index, 0:1, :], slots)
        placing = jnp.where(hit, 1.0, 0.0).astype(BF16)
        gate = jnp.sum(jnp.where(hit, gates[index, 0:1, :], 0.0), axis=1, keepdims=True)
        here = slice(index * slots, (index + 1) * slots)
        rows_ref[here, :] = dot_f32(placing, tok_blocks[index][...]).astype(BF16)
        rows_cot_ref[here, :] = (gate * dot_f32(placing, cot_blocks[index][...])).astype(BF16)
    products = (dot_f32(rows_ref[...], up_ref[...]), dot_f32(rows_cot_ref[...], down_ref[...]))

    @pl.when(step == 0)
    def _():
        for half, product in enumerate(products):
            total[half] = product

    @pl.when(step > 0)
    def _():
        for half, product in enumerate(products):
            total[half] += product

    @pl.when(step == pl.num_programs(0) - 1)
    def _():
        for half in range(2):
            for piece, part_ref in enumerate(part_refs):
                height = part_ref.shape[0]
                rows = slice(piece * height, (piece + 1) * height)
                part_ref[:, half * hidden : (half + 1) * hidden] = total[half, rows].astype(BF16)


def front(blocks, own, capacity, weight_up, weight_down, slots, top_count, pieces):
    tok_rows = blocks[0].shape[0]
    width, hidden = weight_up.shape
    rows = 4 * slots
    tile = width // 2
    weight = pl.BlockSpec((tile, hidden), lambda k: (k, 0))
    picked = pl.BlockSpec((rows, tile), lambda k: (0, k))
    return pl.pallas_call(
        functools.partial(front_kernel, top_count, slots),
        grid=(width // tile,),
        in_specs=[pl.BlockSpec(memory_space=pltpu.SMEM)] * 2
        + [pl.BlockSpec((tok_rows, LANES), lambda k: (0, 2 * width // LANES))] * 4
        + [pl.BlockSpec((tok_rows, tile), lambda k: (0, k))] * 4
        + [pl.BlockSpec((tok_rows, tile), lambda k: (0, width // tile + k))] * 4
        + [weight, weight],
        out_specs=[
            picked,
            picked,
            pl.BlockSpec((4, 8, tok_rows), lambda k: (0, 0, 0)),
        ]
        + [pl.BlockSpec((rows // pieces, 2 * hidden), lambda k: (0, 0))] * pieces,
        out_shape=[
            jax.ShapeDtypeStruct((rows, width), BF16),
            jax.ShapeDtypeStruct((rows, width), BF16),
            jax.ShapeDtypeStruct((4, 8, tok_rows), jnp.int32),
        ]
        + [jax.ShapeDtypeStruct((rows // pieces, 2 * hidden), BF16)] * pieces,
        scratch_shapes=[
            pltpu.VMEM((4, 8, tok_rows), F32),
            pltpu.VMEM((2, rows, hidden), F32),
        ],
        compiler_params=pltpu.CompilerParams(vmem_limit_bytes=32 * 1024 * 1024),
        cost_estimate=NO_COST,
    )(own, capacity, *blocks, *blocks, *blocks, weight_up, weight_down)


def back_kernel(slots, first, slot_ref, part_a, part_b, weight_ref, act_ref, keep_ref, send_ref):
    @pl.when(pl.program_id(0) == 0)
    def _():
        hidden = act_ref.shape[1]
        preact = part_a[:, :hidden].astype(F32) + part_b[:, :hidden].astype(F32)
        hidden_cot = part_a[:, hidden:].astype(F32) + part_b[:, hidden:].astype(F32)
        sigmoid = jax.nn.sigmoid(preact)
        act_ref[...] = (hidden_cot * (sigmoid * (1.0 + preact * (1.0 - sigmoid)))).astype(BF16)

    back = dot_f32(act_ref[...], weight_ref[...], CONTRACT_LAST).astype(BF16)
    for index in range(act_ref.shape[0] // slots):
        hit = placing_of(slot_ref[first + index, 0:1, :], slots)
        placing = jnp.where(hit, 1.0, 0.0).astype(BF16)
        spread = dot_f32(placing, back[index * slots : (index + 1) * slots], CONTRACT_ROWS)
        out_ref = send_ref if index % 2 else keep_ref
        out_ref[index // 2] = spread.astype(BF16)


def back(slot_of, parts, weight, slots, first=0, cost=None):
    tok_rows = slot_of.shape[2]
    width, hidden = weight.shape
    rows = parts[0].shape[0]
    pairs = rows // (2 * slots)
    tile = width // 2
    full = pl.BlockSpec((rows, hidden), lambda n: (0, 0))
    spread = pl.BlockSpec((pairs, tok_rows, tile), lambda n: (0, 0, n))
    return pl.pallas_call(
        functools.partial(back_kernel, slots, first),
        grid=(width // tile,),
        in_specs=[pl.BlockSpec((4, 8, tok_rows), lambda n: (0, 0, 0))]
        + [pl.BlockSpec((rows, 2 * hidden), lambda n: (0, 0))] * 2
        + [pl.BlockSpec((tile, hidden), lambda n: (n, 0))],
        out_specs=[full, spread, spread],
        out_shape=[
            jax.ShapeDtypeStruct((rows, hidden), BF16),
            jax.ShapeDtypeStruct((pairs, tok_rows, width), BF16),
            jax.ShapeDtypeStruct((pairs, tok_rows, width), BF16),
        ],
        compiler_params=pltpu.CompilerParams(vmem_limit_bytes=32 * 1024 * 1024),
        cost_estimate=cost or NO_COST,
    )(slot_of, *parts, weight)


def up_grad_kernel(*refs):
    count = (len(refs) - 1) // 2
    total = None
    for left, right in zip(refs[:count], refs[count:-1]):
        term = dot_f32(left[...], right[...], CONTRACT_ROWS)
        total = term if total is None else total + term
    refs[-1][...] = total.astype(BF16)


def down_grad_kernel(*refs):
    count = (len(refs) - 2) // 3
    out_ref, hidden_ref = refs[-2:]
    heights = [left.shape[0] for left in refs[:count]]
    spans = [slice(sum(heights[:i]), sum(heights[: i + 1])) for i in range(count)]

    @pl.when(pl.program_id(0) == 0)
    def _():
        for span, first, second in zip(spans, refs[count : 2 * count], refs[2 * count : -2]):
            preact = first[...].astype(F32) + second[...].astype(F32)
            hidden_ref[span, :] = (preact * jax.nn.sigmoid(preact)).astype(BF16)

    total = None
    for span, left in zip(spans, refs[:count]):
        term = dot_f32(left[...], hidden_ref[span, :], CONTRACT_ROWS)
        total = term if total is None else total + term
    out_ref[...] = total.astype(BF16)


def weight_grad(kernel, hidden, lefts, pieces, rights, scratch_shapes):
    width = lefts[0].shape[1]
    tile = 256
    in_specs, operands = [], []
    for index, left in enumerate(lefts):
        count = pieces if index == len(lefts) - 1 else 1
        for piece in range(count):
            in_specs.append(pl.BlockSpec((left.shape[0] // count, tile), lambda n, piece=piece: (piece, n)))
            operands.append(left)
    for right in rights:
        in_specs.append(pl.BlockSpec((right.shape[0], hidden), lambda n: (0, 0)))
        operands.append(right)
    return pl.pallas_call(
        kernel,
        grid=(width // tile,),
        in_specs=in_specs,
        out_specs=pl.BlockSpec((tile, hidden), lambda n: (n, 0)),
        out_shape=jax.ShapeDtypeStruct((width, hidden), BF16),
        scratch_shapes=scratch_shapes,
        compiler_params=pltpu.CompilerParams(vmem_limit_bytes=32 * 1024 * 1024),
        cost_estimate=NO_COST,
    )(*operands)


def slots_and_gates(routing, own, limit, top_count):
    ids = routing[:, :, :top_count]
    levels = routing[:, :, top_count:].astype(F32)
    tok_rows = ids.shape[1]
    named = ids == own
    match = jnp.any(named, axis=2)
    gates = jnp.sum(jnp.where(named, levels, 0.0), axis=2) / jnp.sum(levels, axis=2)
    before = jnp.arange(tok_rows)[:, None] < jnp.arange(tok_rows)[None, :]
    rank = dot_f32(match.astype(BF16), before.astype(BF16)).astype(jnp.int32)
    return jnp.where(match & (rank < limit), rank, -1), gates


def grouped(tokens, cotangent, expert_ids, gate_levels, capacity, up_weight, down_weight):
    top_count = expert_ids.shape[1]
    slots = tokens.shape[0] * top_count // capacity.shape[0]
    own = lax.axis_index("expert")
    z = own // (NX * NC)
    inner = (z > 0) & (z < NZ - 1)
    who = own.astype(jnp.int32).reshape(1)
    weight_up, weight_down = up_weight[0], down_weight[0]

    hidden_units = weight_up.shape[1]

    rows_in, rows_cot, slot_of, parts, act, chip = ([None] * NZ for _ in range(6))

    def forth(s, *blocks):
        pieces = 2 if s == NZ - 1 else 1
        rows_in[s], rows_cot[s], slot_of[s], *part = front(
            blocks, who, capacity, weight_up, weight_down, slots, top_count, pieces
        )
        swapped = [swap_dp(part[-1])]
        if pieces == 2:
            swapped.append(swap_dp(tie(part[0], swapped[0])))
        parts[s] = (*part, *swapped)

    def back_again(s, *earlier):
        pair = tie(parts[s], *earlier)
        act[s], keep, send = back(slot_of[s], pair, weight_up, slots)
        chip[s] = add(keep, swap_core(send))

    block = joined(tokens, cotangent, expert_ids, gate_levels)
    x_own = swap_x(block)
    near = along_z(block, NEIGHBOUR)
    two_in = along_z(block, MIDDLE)
    own_core = swap_core(block)

    near, two_in = tie((near, two_in), x_own)
    x_near = swap_x(near)
    far_in = along_z(near, MIDDLE)
    two_out = along_z(two_in, OUTWARD)
    near_core = swap_core(near)
    forth(0, block, own_core, x_own, swap_core(x_own))

    two, two_in, far_in = tie(
        (jnp.where(inner, far_in, two_out), two_in, far_in), x_near, parts[0][0]
    )
    x_two = swap_x(two)
    far_out = along_z(far_in, OUTWARD)
    two_core = swap_core(two)
    forth(1, near, near_core, x_near, swap_core(x_near))

    far = tie(jnp.where(inner, two_in, far_out), x_two, parts[1][0], parts[0][1])
    x_far = swap_x(far)
    far_core = swap_core(far)
    forth(2, two, two_core, x_two, swap_core(x_two))
    back_again(0)

    own_send = tie(chip[0][1], x_far, parts[2][0], parts[1][1])
    back_own = swap_x(own_send)
    forth(3, far, far_core, x_far, swap_core(x_far))
    back_again(1)

    near_send = tie(chip[1][1], back_own, parts[3][0])
    back_near = swap_x(near_send)
    back_again(2)
    near_sum = add(chip[1][0], back_near)
    hop_near = swap_z(near_sum, 1)

    two_send = tie(chip[2][1], near_sum)
    back_two = swap_x(two_send)
    two_sum = add(chip[2][0], back_two)
    hop_two = swap_z(two_sum, 2)
    part_own, part_other, dp_other, dp_own = parts[3]
    act_other, keep, send = back(
        slot_of[3], tie((part_other, dp_other), near_sum, chip[2]), weight_up, slots, 2
    )
    other_sum = add(keep[0], swap_core(send)[0])
    far_send = tie(other_sum, two_sum)
    back_far = swap_x(far_send)
    act_own, keep, send = back(slot_of[3], tie((part_own, dp_own), other_sum), weight_up, slots)
    far_sum = add(add(keep[0], swap_core(tie(send, hop_two, hop_near))[0]), back_far)
    hop_far = swap_z(far_sum, 3)
    whole = parts[:3]
    down_grad = weight_grad(
        down_grad_kernel,
        hidden_units,
        tie(rows_cot, far_sum),
        2,
        [p[0] for p in whole] + [part_own, part_other] + [p[1] for p in whole] + [dp_own, dp_other],
        [pltpu.VMEM((NZ * parts[0][0].shape[0], hidden_units), BF16)],
    )
    up_grad = weight_grad(up_grad_kernel, hidden_units, rows_in, 2, act[:3] + [act_own, act_other], [])
    own_sum = chip[0][0].astype(F32) + back_own.astype(F32)
    for hop in (hop_near, hop_two, hop_far):
        own_sum = own_sum + hop.astype(F32)
    token_grad = own_sum.astype(BF16)
    return token_grad, up_grad[None], down_grad[None]


def general(n_expert, tokens, cotangent, expert_ids, gate_levels, capacity, up_weight, down_weight):
    tok_rows, width = tokens.shape
    top_count = expert_ids.shape[1]
    slots = tok_rows * top_count // capacity.shape[0]
    row_count = n_expert * slots
    own = lax.axis_index("expert")
    weight_up, weight_down = up_weight[0], down_weight[0]

    routing = lax.all_gather(
        jnp.concatenate([expert_ids, gate_levels], axis=1), "expert", axis=0, tiled=False
    )
    tok_all = lax.all_gather(tokens, "expert", axis=0, tiled=False)
    cot_all = lax.all_gather(cotangent, "expert", axis=0, tiled=False)
    slot_of, gates = slots_and_gates(routing, own, capacity[own], top_count)
    placing = slot_of[:, None, :] == jnp.arange(slots, dtype=jnp.int32)[None, :, None]
    slot_gate = jnp.sum(jnp.where(placing, gates[:, None, :], 0.0), axis=2)
    placing = placing.astype(BF16)
    pick = (((2,), (1,)), ((0,), (0,)))
    rows_in = dot_f32(placing, tok_all, pick).astype(BF16).reshape(row_count, width)
    rows_cot = (slot_gate[:, :, None] * dot_f32(placing, cot_all, pick)).astype(BF16)
    rows_cot = rows_cot.reshape(row_count, width)
    preact = lax.psum(dot_f32(rows_in, weight_up).astype(BF16).astype(F32), "dp")
    hidden_cot = lax.psum(dot_f32(rows_cot, weight_down).astype(BF16).astype(F32), "dp")
    sigmoid = jax.nn.sigmoid(preact)
    hidden = (preact * sigmoid).astype(BF16)
    act = (hidden_cot * (sigmoid * (1.0 + preact * (1.0 - sigmoid)))).astype(BF16)
    row_grad = dot_f32(act, weight_up, CONTRACT_LAST).astype(BF16)
    spread = dot_f32(
        placing, row_grad.reshape(n_expert, slots, width), (((1,), (1,)), ((0,), (0,)))
    ).astype(BF16)
    token_grad = lax.psum_scatter(
        spread.reshape(n_expert * tok_rows, width), "expert", scatter_dimension=0, tiled=True
    )
    up_grad = dot_f32(rows_in, act, CONTRACT_ROWS).astype(BF16)[None]
    down_grad = dot_f32(rows_cot, hidden, CONTRACT_ROWS).astype(BF16)[None]
    return token_grad, up_grad, down_grad


def solution(mesh):
    n_dp, n_expert = mesh.shape["dp"], mesh.shape["expert"]
    if n_dp == 2 and n_expert == NZ * NX * NC:
        body = grouped
    else:
        body = functools.partial(general, n_expert)
    return jax.shard_map(
        body,
        mesh=mesh,
        in_specs=(
            P("expert", "dp"),
            P("expert", "dp"),
            P("expert", None),
            P("expert", None),
            P(),
            P("expert", "dp", None),
            P("expert", "dp", None),
        ),
        out_specs=(P("expert", "dp"), P("expert", "dp", None), P("expert", "dp", None)),
        check_vma=False,
    )
```
